256 devices in a mesh: dom: 32 (over y, x, core), sub: 8 (over z).
Axes of the slice: x: 4, y: 4, z: 8, core: 2. Of those that a mesh axis runs over, the one named last changes fastest.
Arguments:
- hamiltonian: bfloat16 [256, 9, 256, 256], P(('dom', 'sub'))
- partitions: int32 [256, 5], P(('dom', 'sub')), may hold values from -1 to 255, as said below
- chemical_potential: float32 [], replicated, may hold values from -0.5 to 0.5
Outputs:
- density: float32 [256, 256, 1280], P(('dom', 'sub'))
- charges: float32 [16384], replicated
The draws below stay inside these ranges and needn't reach their ends.
Inputs may be any that keep to these rules, and one draw needn't show every extreme that they name: `partitions`: slot 0 of each partition is a block owned by the partition's own device (row p lies on device p), each of them once. Slot 1 is -1 or a block of the device one step lower along dom (cyclically) with the same sub index, slot 2 likewise one step higher; slot 3 is -1 or a block of the device one step lower along sub in the same dom group, slot 4 one step higher; no slot 3 exists on the first sub index and no slot 4 on the last. Every halo block lies within 1 of the core block along the second grid dimension and within one along the first. Some partition has all five slots live.
All inputs are finite; a program needn't handle non-finite values.
Results may differ from the reference program's by a relative error of at most 0.0004.
Values may be sent and summed in bfloat16 or wider, within the bound.
No kernel may reach another device: no remote copies, remote signals or barrier semaphores. Data moves between devices by JAX's collectives and lax.ppermute only.
A program may use at most 64 MiB of HBM per device.

```python
import jax
import jax.numpy as jnp
from jax import lax

BLK = 256
ORBS = 4
PART_DEV = 1
REACH = 1
SLOTS = 5
NB = 9
BLOCKS = 256
N_DOM = 32
N_SUB = 8


def draw_hamiltonian(key, part):
    key = jax.random.fold_in(key, 7)
    noise_key, scale_key = jax.random.split(key)
    row_scale = jnp.exp(jax.random.uniform(scale_key, (BLOCKS, 1, BLK, 1), jnp.float32, -1.15, 1.15))
    noise = jnp.clip(jax.random.normal(noise_key, (BLOCKS, NB, BLK, BLK), jnp.float32), -6.0, 6.0)
    return (0.035 * row_scale * noise).astype(jnp.bfloat16)


def pick_between(key, lower, upper):
    spread = jnp.maximum(upper - lower + 1, 1)
    return lower + jax.random.randint(key, lower.shape, 0, 65536, jnp.int32) % spread


def draw_partitions(key, part):
    key = jax.random.fold_in(key, 11)
    keys = jax.random.split(key, 10)
    devices = N_DOM * N_SUB
    device = jnp.arange(devices, dtype=jnp.int32)[:, None]
    scores = jax.random.randint(keys[0], (devices, PART_DEV), 0, 1048576, jnp.int32) * PART_DEV + jnp.arange(PART_DEV, dtype=jnp.int32)[None, :]
    own_slot = jnp.argsort(scores, axis=1, stable=True).astype(jnp.int32)
    dom_index = device // N_SUB
    sub_index = device % N_SUB
    core = device * PART_DEV + own_slot
    near_low = jnp.maximum(own_slot - REACH, 0)
    near_high = jnp.minimum(own_slot + REACH, PART_DEV - 1)
    dom_lower = ((dom_index - 1) % N_DOM * N_SUB + sub_index) * PART_DEV + pick_between(keys[1], near_low, near_high)
    dom_upper = ((dom_index + 1) % N_DOM * N_SUB + sub_index) * PART_DEV + pick_between(keys[2], near_low, near_high)
    low_start = jnp.maximum(own_slot + PART_DEV - REACH, 0)
    sub_lower = (device - 1) * PART_DEV + pick_between(keys[3], low_start, jnp.full_like(own_slot, PART_DEV - 1))
    lower_ok = (sub_index >= 1) & (low_start <= PART_DEV - 1)
    high_end = jnp.minimum(own_slot - PART_DEV + REACH, PART_DEV - 1)
    sub_upper = (device + 1) * PART_DEV + pick_between(keys[4], jnp.zeros_like(own_slot), high_end)
    upper_ok = (sub_index <= N_SUB - 2) & (high_end >= 0)
    forced = (own_slot == 0) & (dom_index == 0) & (sub_index == 1)
    slots = [core]
    candidates = [(dom_lower, True), (dom_upper, True), (sub_lower, lower_ok), (sub_upper, upper_ok)]
    for number, (block_id, allowed) in enumerate(candidates):
        present = (jax.random.randint(keys[5 + number], (devices, PART_DEV), 0, 4, jnp.int32) != 0) | forced
        slots.append(jnp.where(allowed & present, block_id, -1))
    return jnp.stack(slots, axis=-1).reshape(devices * PART_DEV, 5).astype(jnp.int32)


def setup_inputs(seed: int = 0) -> dict:
    streams_of = jax.random.split(jax.random.key(seed), 4)
    hamiltonian = draw_hamiltonian(jax.random.fold_in(streams_of[3], 71), 0)
    partitions = draw_partitions(jax.random.fold_in(streams_of[3], 71), 0)
    chemical_potential = jnp.clip(jax.random.uniform(streams_of[2], (), jnp.float32, -0.5, 0.5), -0.5, 0.5)
    return dict(hamiltonian=hamiltonian, partitions=partitions, chemical_potential=chemical_potential)


def column_blocks(blocks, n_dom, n_sub, part_count):
    span_size = 2 * REACH + 1
    offset = jnp.arange(3 * span_size, dtype=jnp.int32)
    dom_step = offset // span_size - 1
    sub_step = offset % span_size - REACH
    device = blocks // part_count
    dom_coord = device // n_sub
    sub_coord = device % n_sub * part_count + blocks % part_count
    dom_new = (dom_coord[..., None] + dom_step) % n_dom
    sub_new = sub_coord[..., None] + sub_step
    inside = (sub_new >= 0) & (sub_new < n_sub * part_count) & (blocks[..., None] >= 0)
    target = (dom_new * n_sub + sub_new // part_count) * part_count + sub_new % part_count
    return jnp.where(inside, target, -2).astype(jnp.int32)

def density_rows(whole, live_slots, potential):
    sub_order = whole.shape[0]
    orbital_live = jnp.repeat(live_slots.astype(jnp.float32), BLK)
    identity = jnp.eye(sub_order, dtype=jnp.float32)
    symmetric = 0.5 * (whole + whole.T)
    shifted = (potential * identity - symmetric) * orbital_live[:, None] * orbital_live[None, :]
    spectral = 2.0 * jnp.sqrt(jnp.max(lax.optimization_barrier(jnp.sum(shifted * shifted, axis=1))) + 1e-06)
    initial = shifted / spectral
    initial_b = initial.astype(jnp.bfloat16)
    square = jnp.dot(initial_b, initial_b, preferred_element_type=jnp.float32).astype(jnp.bfloat16)
    first_step = 0.5 * (3.0 * initial - jnp.dot(initial_b, square, preferred_element_type=jnp.float32))
    first_b = first_step.astype(jnp.bfloat16)
    square_two = jnp.dot(first_b, first_b, preferred_element_type=jnp.float32).astype(jnp.bfloat16)
    core_rows = 0.5 * (3.0 * first_step[:BLK] - jnp.dot(first_b[:BLK], square_two, preferred_element_type=jnp.float32))
    return 0.5 * (identity[:BLK] + core_rows)

def reference(hamiltonian, partitions, chemical_potential):

    def one_partition(blocks):
        strips = hamiltonian[jnp.maximum(blocks, 0)].astype(jnp.float32)
        columns = column_blocks(blocks, N_DOM, N_SUB, PART_DEV)
        live_slots = blocks >= 0
        matches = (columns[:, :, None] == blocks[None, None, :]) & live_slots[None, None, :] & live_slots[:, None, None]
        whole = jnp.einsum('ikj,ikab->iajb', matches.astype(jnp.float32), strips)
        whole = whole.reshape(SLOTS * BLK, SLOTS * BLK)
        return density_rows(whole, live_slots, chemical_potential)
    density = lax.map(one_partition, partitions)
    diagonal = jnp.diagonal(density[:, :, :BLK], axis1=1, axis2=2)
    charges = 4.0 - 2.0 * lax.optimization_barrier(jnp.sum(diagonal.reshape(BLOCKS * BLK // ORBS, ORBS), axis=1))
    return (density, charges)
```

```python
import functools

import jax
import jax.numpy as jnp
from jax import lax
from jax.experimental import pallas as pl
from jax.experimental.pallas import tpu as pltpu
from jax.sharding import PartitionSpec as P

ORBS = 4
LANES = 128
SLOTS = 5
STEPS = ((0, 0), (-1, 0), (1, 0), (0, -1), (0, 1))
SENT = {1: (4, 7, 6, 8), 2: (4, 1, 0, 2), 3: (4, 5, 2, 8), 4: (4, 3, 0, 6)}


def tile_of(i, j):
    da = STEPS[j][0] - STEPS[i][0]
    db = STEPS[j][1] - STEPS[i][1]
    if abs(da) > 1 or abs(db) > 1:
        return None
    return (da + 1) * 3 + db + 1


COUPLED = {(i, j): tile_of(i, j) is not None for i in range(SLOTS) for j in range(SLOTS)}


def density_kernel(slots, potential, own, r1, r2, r3, r4, density, charges, m, m0, w, wb):
    blk = own.shape[-1]
    f32, bf16 = jnp.float32, jnp.bfloat16
    received = {1: r1, 2: r2, 3: r3, 4: r4}

    def tile(i, j):
        k = tile_of(i, j)
        if i == 0:
            return own[0, k]
        return received[i][0, SENT[i].index(k)]

    def at(i):
        return slice(i * blk, (i + 1) * blk)

    rows = lax.broadcasted_iota(jnp.int32, (blk, blk), 0)
    cols = lax.broadcasted_iota(jnp.int32, (blk, blk), 1)
    eye = rows == cols
    live = [(slots[0, i] >= 0).astype(f32) for i in range(SLOTS)]
    cp = potential[0, 0]

    row_sums = [None] * SLOTS
    col_sums = [None] * SLOTS

    def added(old, new):
        return new if old is None else old + new

    for i in range(SLOTS):
        for j in range(i, SLOTS):
            if not COUPLED[i, j]:
                m[at(i), at(j)] = jnp.zeros((blk, blk), bf16)
                m[at(j), at(i)] = jnp.zeros((blk, blk), bf16)
                continue
            both = tile(i, j).astype(f32) + tile(j, i).T.astype(f32)
            if i == j:
                block = (jnp.where(eye, cp, 0.0) - 0.5 * both) * live[i]
            else:
                block = both * (-0.5 * live[i] * live[j])
            squares = block * block
            row_sums[i] = added(row_sums[i], jnp.sum(squares, axis=1, keepdims=True))
            rounded = block.astype(bf16)
            m[at(i), at(j)] = rounded
            if i == 0:
                m0[:, at(j)] = block
            if i != j:
                col_sums[j] = added(col_sums[j], jnp.sum(squares, axis=0, keepdims=True))
                m[at(j), at(i)] = rounded.T
    largest = jnp.max(row_sums[0], axis=0, keepdims=True)
    for j in range(1, SLOTS):
        turned = jnp.sum(jnp.where(eye, col_sums[j], 0.0), axis=1, keepdims=True)
        largest = jnp.maximum(largest, jnp.max(row_sums[j] + turned, axis=0, keepdims=True))
    inv = 1.0 / (2.0 * jnp.sqrt(largest + 1e-06))

    for i in range(SLOTS):
        for j in range(i, SLOTS):
            total = None
            for k in range(SLOTS):
                if COUPLED[i, k] and COUPLED[k, j]:
                    term = jnp.dot(m[at(i), at(k)], m[at(k), at(j)], preferred_element_type=f32)
                    total = added(total, term)
            w[at(i), at(j)] = total
    for i in range(SLOTS):
        for j in range(i, SLOTS):
            rounded = (w[at(i), at(j)] * inv * inv).astype(bf16)
            wb[at(i), at(j)] = rounded
            if i != j:
                wb[at(j), at(i)] = rounded.T

    def times_w(left, j):
        return jnp.dot(left, wb[:, at(j)], preferred_element_type=f32)

    def join(parts):
        return jnp.concatenate(parts, axis=1)

    left = m[at(0), :]
    first = [
        inv * (1.5 * m0[:, at(j)] - 0.5 * times_w(left, j)) for j in range(SLOTS)
    ]
    left = join([part.astype(bf16) for part in first])
    for j in range(SLOTS):
        m0[:, at(j)] = first[j]
    second = [times_w(left, j) for j in range(SLOTS)]
    left = join([part.astype(bf16) for part in second])
    third = [1.5 * second[j] - 0.5 * times_w(left, j) for j in range(SLOTS)]
    left = join([part.astype(bf16) for part in third])
    for j in range(SLOTS):
        sign = 1.5 * m0[:, at(j)] - 0.75 * third[j] + 0.25 * times_w(left, j)
        if j == 0:
            sign = jnp.where(eye, 1.0 + sign, sign)
        density[0, :, at(j)] = 0.5 * sign
    occupied = jnp.sum(jnp.where(eye, density[0, :, at(0)], 0.0), axis=1, keepdims=True)
    copies, height, lanes = charges.shape
    atoms = blk // ORBS
    place = slots[0, 0] % copies * atoms
    atom = lax.broadcasted_iota(jnp.int32, (blk, lanes), 0) // ORBS + place % lanes
    lane = lax.broadcasted_iota(jnp.int32, (blk, lanes), 1)
    held = jnp.sum(jnp.where(atom == lane, 4.0 / ORBS - 2.0 * occupied, 0.0), axis=0, keepdims=True)
    row = lax.broadcasted_iota(jnp.int32, (height, lanes), 0)
    placed = jnp.where(row == place // lanes, held, 0.0)
    for copy in range(copies):
        charges[copy] = placed


def pack_kernel(slots, own, earlier, *refs):
    packs, sems = refs[:-1], refs[-1]
    copies = []
    for place, slot in enumerate(slots):
        for index, k in enumerate(SENT[slot]):
            copies.append(
                pltpu.make_async_copy(
                    own.at[0, k], packs[place].at[0, index], sems.at[len(copies)]
                )
            )
    for copy in copies:
        copy.start()
    for copy in copies:
        copy.wait()


def packed(own, earlier, *slots):
    blk = own.shape[-1]
    anywhere = pl.BlockSpec(memory_space=pl.ANY)
    shape = jax.ShapeDtypeStruct((1, len(SENT[1]), blk, blk), own.dtype)
    return pl.pallas_call(
        functools.partial(pack_kernel, slots),
        out_shape=(shape,) * len(slots),
        in_specs=[pl.BlockSpec(memory_space=pltpu.HBM), anywhere],
        out_specs=(anywhere,) * len(slots),
        scratch_shapes=[pltpu.SemaphoreType.DMA((len(slots) * len(SENT[1]),))],
        name="pack_halo",
    )(own, earlier)


def local_part(slots, potential, own, received, n_sub):
    blk = own.shape[-1]
    order = SLOTS * blk
    vmem = pl.BlockSpec(memory_space=pltpu.VMEM)
    smem = pl.BlockSpec(memory_space=pltpu.SMEM)
    return pl.pallas_call(
        density_kernel,
        out_shape=(
            jax.ShapeDtypeStruct((1, blk, order), jnp.float32),
            jax.ShapeDtypeStruct((n_sub, 8, LANES), jnp.float32),
        ),
        in_specs=[smem, smem] + [vmem] * 5,
        out_specs=(vmem, vmem),
        scratch_shapes=[
            pltpu.VMEM((order, order), jnp.bfloat16),
            pltpu.VMEM((blk, order), jnp.float32),
            pltpu.VMEM((order, order), jnp.float32),
            pltpu.VMEM((order, order), jnp.bfloat16),
        ],
        compiler_params=pltpu.CompilerParams(vmem_limit_bytes=48 * 1024 * 1024),
        name="density_rows",
    )(slots, potential, own, *received)


def shards(hamiltonian, partitions, chemical_potential):
    n_dom = lax.axis_size("dom")
    n_sub = lax.axis_size("sub")
    blk = hamiltonian.shape[2]

    def exchanged(up, down, axis, size):
        forward = [(i, (i + 1) % size) for i in range(size)]
        return (
            lax.ppermute(up, axis, forward),
            lax.ppermute(down, axis, [(j, i) for i, j in forward]),
        )

    sub_up, sub_down = packed(hamiltonian, partitions, 3, 4)
    dom_up, dom_down = packed(hamiltonian, sub_up, 1, 2)
    r3, r4 = exchanged(sub_up, sub_down, "sub", n_sub)
    r1, r2 = exchanged(dom_up, dom_down, "dom", n_dom)
    density, placed = local_part(
        partitions, chemical_potential.reshape(1, 1), hamiltonian, (r1, r2, r3, r4), n_sub
    )
    group_rows = n_sub * blk // ORBS // LANES
    by_sub = lax.all_to_all(placed, "sub", 0, 0, tiled=True)
    group = jnp.sum(by_sub, axis=0)[:group_rows]
    copies = jnp.broadcast_to(group[None], (n_dom, group_rows, LANES))
    charges = lax.all_to_all(copies, "dom", 0, 0, tiled=True).reshape(-1)
    return (density, charges)


def solution(mesh):
    return jax.shard_map(
        shards,
        mesh=mesh,
        in_specs=(P(("dom", "sub"), None, None, None), P(("dom", "sub"), None), P()),
        out_specs=(P(("dom", "sub"), None, None), P()),
        check_vma=False,
    )
```

```python
import functools

import jax
import jax.numpy as jnp
from jax import lax
from jax.experimental import pallas as pl
from jax.experimental.pallas import tpu as pltpu
from jax.sharding import PartitionSpec as P

ORBS = 4
LANES = 128
SLOTS = 5
STEPS = ((0, 0), (-1, 0), (1, 0), (0, -1), (0, 1))
SENT = {1: (4, 7, 6, 8), 2: (4, 1, 0, 2), 3: (4, 5, 2, 8), 4: (4, 3, 0, 6)}


def tile_of(i, j):
    da = STEPS[j][0] - STEPS[i][0]
    db = STEPS[j][1] - STEPS[i][1]
    if abs(da) > 1 or abs(db) > 1:
        return None
    return (da + 1) * 3 + db + 1


COUPLED = {(i, j): tile_of(i, j) is not None for i in range(SLOTS) for j in range(SLOTS)}


def density_kernel(
    slots, potential, own, r1, r2, r3, r4, density, charges, x0, x0b, q0b, x1b
):
    blk = own.shape[-1]
    f32, bf16 = jnp.float32, jnp.bfloat16
    received = {1: r1, 2: r2, 3: r3, 4: r4}
    upper = [(i, j) for i in range(SLOTS) for j in range(i, SLOTS)]

    def tile(i, j):
        k = tile_of(i, j)
        if i == 0:
            return own[0, k]
        return received[i][0, SENT[i].index(k)]

    def at(i):
        return slice(i * blk, (i + 1) * blk)

    def product(left, right, i, j):
        total = None
        for k in range(SLOTS):
            if left is x0b and not COUPLED[i, k] or right is x0b and not COUPLED[k, j]:
                continue
            term = jnp.dot(left[at(i), at(k)], right[at(k), at(j)], preferred_element_type=f32)
            total = added(total, term)
        return total

    def mirror(target, i, j, block):
        rounded = block.astype(bf16)
        target[at(i), at(j)] = rounded
        if i != j:
            target[at(j), at(i)] = rounded.T

    def added(old, new):
        return new if old is None else old + new

    rows = lax.broadcasted_iota(jnp.int32, (blk, blk), 0)
    cols = lax.broadcasted_iota(jnp.int32, (blk, blk), 1)
    eye = rows == cols
    live = [(slots[0, i] >= 0).astype(f32) for i in range(SLOTS)]
    cp = potential[0, 0]

    row_sums = [None] * SLOTS
    col_sums = [None] * SLOTS
    for i, j in upper:
        if not COUPLED[i, j]:
            continue
        both = tile(i, j).astype(f32) + tile(j, i).T.astype(f32)
        if i == j:
            block = (jnp.where(eye, cp, 0.0) - 0.5 * both) * live[i]
        else:
            block = both * (-0.5 * live[i] * live[j])
        x0[at(i), at(j)] = block
        squares = block * block
        row_sums[i] = added(row_sums[i], jnp.sum(squares, axis=1, keepdims=True))
        if i != j:
            col_sums[j] = added(col_sums[j], jnp.sum(squares, axis=0, keepdims=True))
    largest = jnp.max(row_sums[0], axis=0, keepdims=True)
    for j in range(1, SLOTS):
        turned = jnp.sum(jnp.where(eye, col_sums[j], 0.0), axis=1, keepdims=True)
        largest = jnp.maximum(largest, jnp.max(row_sums[j] + turned, axis=0, keepdims=True))
    inv = 1.0 / (2.0 * jnp.sqrt(largest + 1e-06))

    for i, j in upper:
        if COUPLED[i, j]:
            block = x0[at(i), at(j)] * inv
            x0[at(i), at(j)] = block
            mirror(x0b, i, j, block)
    for i, j in upper:
        mirror(q0b, i, j, product(x0b, x0b, i, j))
    first = []
    for i, j in upper:
        block = -0.5 * product(x0b, q0b, i, j)
        if COUPLED[i, j]:
            block = 1.5 * x0[at(i), at(j)] + block
        if i == 0:
            first.append(block)
        mirror(x1b, i, j, block)
    for j in range(SLOTS):
        x0[at(0), at(j)] = first[j]
    left = jnp.concatenate(
        [
            jnp.dot(x1b[at(0), :], x1b[:, at(j)], preferred_element_type=f32).astype(bf16)
            for j in range(SLOTS)
        ],
        axis=1,
    )
    for j in range(SLOTS):
        sign = 1.5 * x0[at(0), at(j)] - 0.5 * jnp.dot(
            left, x1b[:, at(j)], preferred_element_type=f32
        )
        if j == 0:
            sign = jnp.where(eye, 1.0 + sign, sign)
        density[0, :, at(j)] = 0.5 * sign
    occupied = jnp.sum(jnp.where(eye, density[0, :, at(0)], 0.0), axis=1, keepdims=True)
    lanes = charges.shape[1]
    atoms = blk // ORBS
    atom = lax.broadcasted_iota(jnp.int32, (blk, lanes), 0) // ORBS + slots[0, 0] % 2 * atoms
    lane = lax.broadcasted_iota(jnp.int32, (blk, lanes), 1)
    charges[...] = jnp.sum(
        jnp.where(atom == lane, 4.0 / ORBS - 2.0 * occupied, 0.0), axis=0, keepdims=True
    )


def pack_kernel(slots, own, earlier, *packs):
    for slot, pack in zip(slots, packs):
        for index, k in enumerate(SENT[slot]):
            pack[0, index] = own[0, k]


def packed(own, earlier, *slots):
    blk = own.shape[-1]
    vmem = pl.BlockSpec(memory_space=pltpu.VMEM)
    shape = jax.ShapeDtypeStruct((1, len(SENT[1]), blk, blk), own.dtype)
    return pl.pallas_call(
        functools.partial(pack_kernel, slots),
        out_shape=(shape,) * len(slots),
        in_specs=[vmem, pl.BlockSpec(memory_space=pl.ANY)],
        out_specs=(vmem,) * len(slots),
        name="pack_halo",
    )(own, earlier)


def order_kernel(slots, rows, out):
    device = slots[0, 0]
    y, x, core, high = device // 64, device // 16 % 4, device // 8 % 2, device // 2 % 4
    for dy in range(4):
        for dx in range(4):
            for dcore in range(2):
                for dhigh in range(4):
                    source = ((dhigh * 4 + dy) * 4 + dx) * 2 + dcore
                    target = ((lax.rem(y + 4 - dy, 4) * 4 + lax.rem(x + 4 - dx, 4)) * 2
                              + lax.rem(core + dcore, 2)) * 4 + lax.rem(high + 4 - dhigh, 4)
                    out[pl.ds(target, 1), :] = rows[source : source + 1, :]


def in_order(slots, rows):
    return pl.pallas_call(
        order_kernel,
        out_shape=jax.ShapeDtypeStruct(rows.shape, rows.dtype),
        in_specs=[
            pl.BlockSpec(memory_space=pltpu.SMEM),
            pl.BlockSpec(memory_space=pltpu.VMEM),
        ],
        out_specs=pl.BlockSpec(memory_space=pltpu.VMEM),
        name="order_charges",
    )(slots, rows)


def moved(x, n_dom, n_sub, dy, dx, flip_core, dz, flip_z):
    pairs = []
    for d in range(n_dom):
        for z in range(n_sub):
            y, col, core = d // 8, d // 2 % 4, d % 2
            to = (((y + dy) % 4 * 4 + (col + dx) % 4) * 2 + (core ^ flip_core)) * n_sub
            pairs.append((d * n_sub + z, to + ((z + dz) % n_sub ^ flip_z)))
    return lax.ppermute(x, ("dom", "sub"), pairs)


def gathered(row, n_dom, n_sub):
    def step(x, *where):
        return moved(x, n_dom, n_sub, *where)

    here = row + step(row, 0, 0, 0, 0, 1)
    there = step(row, 0, 0, 1, 0, 0) + step(row, 0, 0, 1, 0, 1)
    block = jnp.concatenate([here, there], axis=0)
    block = jnp.concatenate([block] + [step(block, 0, d, 0, 0, 0) for d in (1, 2, 3)], axis=0)
    block = jnp.concatenate([block] + [step(block, d, 0, 0, 0, 0) for d in (1, 2, 3)], axis=0)
    return jnp.concatenate([block] + [step(block, 0, 0, 0, 2 * d, 0) for d in (1, 2, 3)], axis=0)


def local_part(slots, potential, own, received):
    blk = own.shape[-1]
    order = SLOTS * blk
    vmem = pl.BlockSpec(memory_space=pltpu.VMEM)
    smem = pl.BlockSpec(memory_space=pltpu.SMEM)
    return pl.pallas_call(
        density_kernel,
        out_shape=(
            jax.ShapeDtypeStruct((1, blk, order), jnp.float32),
            jax.ShapeDtypeStruct((1, LANES), jnp.float32),
        ),
        in_specs=[smem, smem] + [vmem] * 5,
        out_specs=(vmem, vmem),
        scratch_shapes=[
            pltpu.VMEM((order, order), jnp.float32),
            pltpu.VMEM((order, order), jnp.bfloat16),
            pltpu.VMEM((order, order), jnp.bfloat16),
            pltpu.VMEM((order, order), jnp.bfloat16),
        ],
        compiler_params=pltpu.CompilerParams(vmem_limit_bytes=48 * 1024 * 1024),
        name="density_rows",
    )(slots, potential, own, *received)


def shards(hamiltonian, partitions, chemical_potential):
    n_dom = lax.axis_size("dom")
    n_sub = lax.axis_size("sub")
    blk = hamiltonian.shape[2]

    def exchanged(up, down, axis, size):
        forward = [(i, (i + 1) % size) for i in range(size)]
        return (
            lax.ppermute(up, axis, forward),
            lax.ppermute(down, axis, [(j, i) for i, j in forward]),
        )

    sub_up, sub_down = packed(hamiltonian, partitions, 3, 4)
    dom_up, dom_down = packed(hamiltonian, sub_up, 1, 2)
    r3, r4 = exchanged(sub_up, sub_down, "sub", n_sub)
    r1, r2 = exchanged(dom_up, dom_down, "dom", n_dom)
    density, row = local_part(
        partitions, chemical_potential.reshape(1, 1), hamiltonian, (r1, r2, r3, r4)
    )
    charges = in_order(partitions, gathered(row, n_dom, n_sub)).reshape(-1)
    return (density, charges)


def solution(mesh):
    return jax.shard_map(
        shards,
        mesh=mesh,
        in_specs=(P(("dom", "sub"), None, None, None), P(("dom", "sub"), None), P()),
        out_specs=(P(("dom", "sub"), None, None), P()),
        check_vma=False,
    )
```

```python
import functools

import jax
import jax.numpy as jnp
from jax import lax
from jax.experimental import pallas as pl
from jax.experimental.pallas import tpu as pltpu
from jax.sharding import PartitionSpec as P

ORBS = 4
SLOTS = 5
LANES = 128
MIB = 1024 * 1024
STEPS = ((0, 0), (-1, 0), (1, 0), (0, -1), (0, 1))
SENT = {1: (4, 7, 6, 8), 2: (4, 1, 0, 2), 3: (4, 5, 2, 8), 4: (4, 3, 0, 6)}
ORDER = (0, 3, 4, 1, 2)
EARLY = (0, 1, 2)


def tile_of(i, j):
    da = STEPS[j][0] - STEPS[i][0]
    db = STEPS[j][1] - STEPS[i][1]
    if abs(da) > 1 or abs(db) > 1:
        return None
    return (da + 1) * 3 + db + 1


PAIRS = [
    (ORDER[p], ORDER[q])
    for p in range(SLOTS)
    for q in range(p, SLOTS)
    if tile_of(ORDER[p], ORDER[q]) is not None
]
EARLY_PAIRS = [pair for pair in PAIRS if pair[0] in EARLY and pair[1] in EARLY]
LATE_PAIRS = [pair for pair in PAIRS if pair not in EARLY_PAIRS]
TURNED = [(i, j) for i, j in LATE_PAIRS if j in EARLY]


def runs(blocks):
    found = []
    for k in blocks:
        if found and found[-1][1] == k:
            found[-1][1] = k + 1
        else:
            found.append([k, k + 1])
    return found


def added(old, new):
    return new if old is None else old + new


class Halo:
    def __init__(self, slots, potential, own, received):
        self.own, self.received = own, received
        blk = own.shape[-1]
        rows = lax.broadcasted_iota(jnp.int32, (blk, blk), 0)
        self.eye = rows == lax.broadcasted_iota(jnp.int32, (blk, blk), 1)
        self.live = [(slots[0, i] >= 0).astype(jnp.float32) for i in range(SLOTS)]
        self.potential = potential[0, 0]
        self.row_sums = [None] * SLOTS
        self.col_sums = [None] * SLOTS

    def tile(self, i, j):
        k = tile_of(i, j)
        if i == 0:
            return self.own[0, k]
        parts = self.received[i]
        place = SENT[i].index(k)
        return parts[place // parts[0].shape[1]][0, place % parts[0].shape[1]]

    def block(self, i, j, turned=None):
        if turned is None:
            turned = self.tile(j, i).T
        both = self.tile(i, j).astype(jnp.float32) + turned.astype(jnp.float32)
        if i == j:
            block = (jnp.where(self.eye, self.potential, 0.0) - 0.5 * both) * self.live[i]
        else:
            block = both * (-0.5 * self.live[i] * self.live[j])
        squares = block * block
        folded = squares[:, :LANES]
        for lane in range(LANES, squares.shape[1], LANES):
            folded = folded + squares[:, lane : lane + LANES]
        self.row_sums[i] = added(self.row_sums[i], folded)
        if i != j:
            self.col_sums[j] = added(self.col_sums[j], jnp.sum(squares, axis=0, keepdims=True))
        return block

    def sums(self, i):
        total = self.row_sums[i]
        if total is not None:
            total = jnp.sum(total, axis=1, keepdims=True)
        if self.col_sums[i] is not None:
            turned = jnp.sum(jnp.where(self.eye, self.col_sums[i], 0.0), axis=1, keepdims=True)
            total = added(total, turned)
        return total


def early_kernel(slots, potential, own, r1a, r1b, r2a, r2b, blocks, turned, sums):
    halo = Halo(slots, potential, own, {1: (r1a, r1b), 2: (r2a, r2b)})
    for place, (i, j) in enumerate(TURNED):
        turned[place] = halo.tile(j, i).T
    for place, (i, j) in enumerate(EARLY_PAIRS):
        blocks[place] = halo.block(i, j)
    lane = lax.broadcasted_iota(jnp.int32, sums.shape, 1)
    total = jnp.zeros(sums.shape, jnp.float32)
    for i in EARLY:
        total = jnp.where(lane == i, halo.sums(i), total)
    sums[...] = total


def late_kernel(
    slots, potential, own, early, turned, sums, r3, r4, density, charges,
    x0, x0b, q0b, x1b, out, sems,
):
    blk = own.shape[-1]
    f32, bf16 = jnp.float32, jnp.bfloat16
    halo = Halo(slots, potential, own, {3: (r3,), 4: (r4,)})
    eye = halo.eye

    def at(p, q=None):
        return slice(p * blk, (p + 1 if q is None else q) * blk)

    def coupled(p, q):
        return tile_of(ORDER[p], ORDER[q]) is not None

    def product(left, right, p, q):
        inner = [
            k for k in range(SLOTS)
            if (left is not x0b or coupled(p, k)) and (right is not x0b or coupled(k, q))
        ]
        total = None
        for lo, hi in runs(inner):
            term = jnp.dot(left[at(p), at(lo, hi)], right[at(lo, hi), at(q)], preferred_element_type=f32)
            total = added(total, term)
        return total

    def mirror(target, p, q, block):
        rounded = block.astype(bf16)
        target[at(p), at(q)] = rounded
        if p != q:
            target[at(q), at(p)] = rounded.T

    def place(i, j):
        return ORDER.index(i), ORDER.index(j)

    for i, j in LATE_PAIRS:
        p, q = place(i, j)
        x0[at(p), at(q)] = halo.block(i, j, turned[TURNED.index((i, j))] if (i, j) in TURNED else None)
    largest = None
    for i in range(SLOTS):
        total = halo.sums(i)
        if i in EARLY:
            total = added(sums[:, i : i + 1], total) if total is not None else sums[:, i : i + 1]
        top = jnp.max(total, axis=0, keepdims=True)
        largest = top if largest is None else jnp.maximum(largest, top)
    inv = 1.0 / (2.0 * jnp.sqrt(largest + 1e-06))

    for i, j in PAIRS:
        p, q = place(i, j)
        if (i, j) in EARLY_PAIRS:
            block = early[EARLY_PAIRS.index((i, j))] * inv
        else:
            block = x0[at(p), at(q)] * inv
        x0[at(p), at(q)] = block
        mirror(x0b, p, q, block)
    upper = [(p, q) for p in range(SLOTS) for q in range(p, SLOTS)]
    for p, q in upper:
        mirror(q0b, p, q, product(x0b, x0b, p, q))
    for p, q in upper:
        block = -0.5 * product(x0b, q0b, p, q)
        if coupled(p, q):
            block = 1.5 * x0[at(p), at(q)] + block
        if p == 0:
            x0[at(0), at(q)] = block
        mirror(x1b, p, q, block)
    left = jnp.concatenate(
        [product(x1b, x1b, 0, q).astype(bf16) for q in range(SLOTS)], axis=1
    )
    copies = []
    for q in range(SLOTS):
        sign = 1.5 * x0[at(0), at(q)] - 0.5 * jnp.dot(
            left, x1b[:, at(q)], preferred_element_type=f32
        )
        if q == 0:
            sign = jnp.where(eye, 1.0 + sign, sign)
        result = 0.5 * sign
        out[q] = result
        copy = pltpu.make_async_copy(
            out.at[q], density.at[0, :, pl.ds(ORDER[q] * blk, blk)], sems.at[q]
        )
        copy.start()
        copies.append(copy)
        if q == 0:
            occupied = jnp.sum(jnp.where(eye, result, 0.0), axis=1, keepdims=True)
            lanes = charges.shape[1]
            atoms = blk // ORBS
            atom = lax.broadcasted_iota(jnp.int32, (blk, lanes), 0) // ORBS + slots[0, 0] % 2 * atoms
            lane = lax.broadcasted_iota(jnp.int32, (blk, lanes), 1)
            charges[...] = jnp.sum(
                jnp.where(atom == lane, 4.0 / ORBS - 2.0 * occupied, 0.0), axis=0, keepdims=True
            )
    for copy in copies:
        copy.wait()


VMEM = pl.BlockSpec(memory_space=pltpu.VMEM)
SMEM = pl.BlockSpec(memory_space=pltpu.SMEM)
ANY = pl.BlockSpec(memory_space=pl.ANY)


SMALL = pl.CostEstimate(flops=1, bytes_accessed=1, transcendentals=0)


def limit(mib):
    return pltpu.CompilerParams(vmem_limit_bytes=mib * MIB)


def early_part(slots, potential, own, *halves):
    blk = own.shape[-1]
    return pl.pallas_call(
        early_kernel,
        out_shape=(
            jax.ShapeDtypeStruct((len(EARLY_PAIRS), blk, blk), jnp.float32),
            jax.ShapeDtypeStruct((len(TURNED), blk, blk), own.dtype),
            jax.ShapeDtypeStruct((blk, LANES), jnp.float32),
        ),
        in_specs=[SMEM, SMEM] + [VMEM] * 5,
        out_specs=(VMEM, VMEM, VMEM),
        compiler_params=limit(12),
        cost_estimate=SMALL,
        name="early_blocks",
    )(slots, potential, own, *halves)


def late_part(slots, potential, own, early, turned, sums, r3, r4):
    blk = own.shape[-1]
    order = SLOTS * blk
    return pl.pallas_call(
        late_kernel,
        out_shape=(
            jax.ShapeDtypeStruct((1, blk, order), jnp.float32),
            jax.ShapeDtypeStruct((1, LANES), jnp.float32),
        ),
        in_specs=[SMEM, SMEM] + [VMEM] * 6,
        out_specs=(ANY, VMEM),
        scratch_shapes=[
            pltpu.VMEM((order, order), jnp.float32),
            pltpu.VMEM((order, order), jnp.bfloat16),
            pltpu.VMEM((order, order), jnp.bfloat16),
            pltpu.VMEM((order, order), jnp.bfloat16),
            pltpu.VMEM((SLOTS, blk, blk), jnp.float32),
            pltpu.SemaphoreType.DMA((SLOTS,)),
        ],
        compiler_params=limit(32),
        name="density_rows",
    )(slots, potential, own, early, turned, sums, r3, r4)


def pack_kernel(groups, own, earlier, *packs):
    for group, pack in zip(groups, packs):
        for index, k in enumerate(group):
            pack[0, index] = own[0, k]


def packed(own, earlier, *groups):
    blk = own.shape[-1]
    return pl.pallas_call(
        functools.partial(pack_kernel, groups),
        out_shape=tuple(
            jax.ShapeDtypeStruct((1, len(group), blk, blk), own.dtype) for group in groups
        ),
        in_specs=[VMEM, ANY],
        out_specs=(VMEM,) * len(groups),
        compiler_params=limit(4),
        cost_estimate=SMALL,
        name="pack_halo",
    )(own, earlier)


def pair_kernel(rows, out):
    half = out.shape[0]
    out[...] = rows[pl.ds(0, half, stride=2), :] + rows[pl.ds(1, half, stride=2), :]


def paired(rows):
    return pl.pallas_call(
        pair_kernel,
        out_shape=jax.ShapeDtypeStruct((rows.shape[0] // 2, rows.shape[1]), rows.dtype),
        in_specs=[VMEM],
        out_specs=VMEM,
        compiler_params=limit(2),
        name="pair_charges",
    )(rows)


def shards(hamiltonian, partitions, chemical_potential):
    n_dom = lax.axis_size("dom")
    n_sub = lax.axis_size("sub")
    potential = chemical_potential.reshape(1, 1)

    def up(x, axis, size):
        return lax.ppermute(x, axis, [(i, (i + 1) % size) for i in range(size)])

    def down(x, axis, size):
        return lax.ppermute(x, axis, [((i + 1) % size, i) for i in range(size)])

    sub_up, sub_down = packed(hamiltonian, hamiltonian, SENT[3], SENT[4])
    dom_parts = packed(
        hamiltonian, sub_up, SENT[1][:2], SENT[1][2:], SENT[2][:2], SENT[2][2:]
    )
    r3, r4 = up(sub_up, "sub", n_sub), down(sub_down, "sub", n_sub)
    halves = [up(x, "dom", n_dom) for x in dom_parts[:2]]
    halves += [down(x, "dom", n_dom) for x in dom_parts[2:]]
    early, turned, sums = early_part(partitions, potential, hamiltonian, *halves)
    density, row = late_part(
        partitions, potential, hamiltonian, early, turned, sums, r3, r4
    )
    copies = jnp.broadcast_to(row, (n_dom * n_sub, LANES))
    rows = lax.all_to_all(copies, ("dom", "sub"), 0, 0, tiled=True)
    charges = paired(rows).reshape(-1)
    return (density, charges)


def solution(mesh):
    return jax.shard_map(
        shards,
        mesh=mesh,
        in_specs=(P(("dom", "sub"), None, None, None), P(("dom", "sub"), None), P()),
        out_specs=(P(("dom", "sub"), None, None), P()),
        check_vma=False,
    )
```

```python
import functools

import jax
import jax.numpy as jnp
from jax import lax
from jax.experimental import pallas as pl
from jax.experimental.pallas import tpu as pltpu
from jax.sharding import PartitionSpec as P

ORBS = 4
SLOTS = 5
LANES = 128
MIB = 1024 * 1024
STEPS = ((0, 0), (-1, 0), (1, 0), (0, -1), (0, 1))
SENT = {1: (4, 7, 6, 8), 2: (4, 1, 0, 2), 3: (4, 5, 2, 8), 4: (4, 3, 0, 6)}
ORDER = (0, 3, 4, 1, 2)
EARLY = (0, 1, 2)


def tile_of(i, j):
    da = STEPS[j][0] - STEPS[i][0]
    db = STEPS[j][1] - STEPS[i][1]
    if abs(da) > 1 or abs(db) > 1:
        return None
    return (da + 1) * 3 + db + 1


PAIRS = [
    (ORDER[p], ORDER[q])
    for p in range(SLOTS)
    for q in range(p, SLOTS)
    if tile_of(ORDER[p], ORDER[q]) is not None
]
EARLY_PAIRS = [pair for pair in PAIRS if pair[0] in EARLY and pair[1] in EARLY]
LATE_PAIRS = [pair for pair in PAIRS if pair not in EARLY_PAIRS]
TURNED = [(i, j) for i, j in LATE_PAIRS if j in EARLY]


def runs(blocks):
    found = []
    for k in blocks:
        if found and found[-1][1] == k:
            found[-1][1] = k + 1
        else:
            found.append([k, k + 1])
    return found


def added(old, new):
    return new if old is None else old + new


class Halo:
    def __init__(self, slots, potential, own, received):
        self.own, self.received = own, received
        blk = own.shape[-1]
        rows = lax.broadcasted_iota(jnp.int32, (blk, blk), 0)
        self.eye = rows == lax.broadcasted_iota(jnp.int32, (blk, blk), 1)
        self.live = [(slots[0, i] >= 0).astype(jnp.float32) for i in range(SLOTS)]
        self.potential = potential[0, 0]
        self.row_sums = [None] * SLOTS
        self.col_sums = [None] * SLOTS

    def tile(self, i, j):
        k = tile_of(i, j)
        if i == 0:
            return self.own[0, k]
        parts = self.received[i]
        place = SENT[i].index(k)
        return parts[place // parts[0].shape[1]][0, place % parts[0].shape[1]]

    def block(self, i, j, turned=None):
        if turned is None:
            turned = self.tile(j, i).T
        both = self.tile(i, j).astype(jnp.float32) + turned.astype(jnp.float32)
        if i == j:
            block = (jnp.where(self.eye, self.potential, 0.0) - 0.5 * both) * self.live[i]
        else:
            block = both * (-0.5 * self.live[i] * self.live[j])
        squares = block * block
        folded = squares[:, :LANES]
        for lane in range(LANES, squares.shape[1], LANES):
            folded = folded + squares[:, lane : lane + LANES]
        self.row_sums[i] = added(self.row_sums[i], folded)
        if i != j:
            self.col_sums[j] = added(self.col_sums[j], jnp.sum(squares, axis=0, keepdims=True))
        return block

    def sums(self, i):
        total = self.row_sums[i]
        if total is not None:
            total = jnp.sum(total, axis=1, keepdims=True)
        if self.col_sums[i] is not None:
            turned = jnp.sum(jnp.where(self.eye, self.col_sums[i], 0.0), axis=1, keepdims=True)
            total = added(total, turned)
        return total


def early_kernel(slots, potential, own, r1a, r1b, r2a, r2b, blocks, turned, sums):
    halo = Halo(slots, potential, own, {1: (r1a, r1b), 2: (r2a, r2b)})
    for place, (i, j) in enumerate(TURNED):
        turned[place] = halo.tile(j, i).T
    for place, (i, j) in enumerate(EARLY_PAIRS):
        blocks[place] = halo.block(i, j)
    lane = lax.broadcasted_iota(jnp.int32, sums.shape, 1)
    total = jnp.zeros(sums.shape, jnp.float32)
    for i in EARLY:
        total = jnp.where(lane == i, halo.sums(i), total)
    sums[...] = total


def late_kernel(
    slots, potential, own, early, turned, sums, r4, r3,
    charges, core, first, y, x1b, x0, x0b, q0b,
):
    blk = own.shape[-1]
    f32, bf16 = jnp.float32, jnp.bfloat16
    halo = Halo(slots, potential, own, {3: (r3,), 4: (r4,)})
    eye = halo.eye

    def at(p, q=None):
        return slice(p * blk, (p + 1 if q is None else q) * blk)

    def coupled(p, q):
        return tile_of(ORDER[p], ORDER[q]) is not None

    def product(left, right, p, q):
        inner = [
            k for k in range(SLOTS)
            if (left is not x0b or coupled(p, k)) and (right is not x0b or coupled(k, q))
        ]
        total = None
        for lo, hi in runs(inner):
            term = jnp.dot(left[at(p), at(lo, hi)], right[at(lo, hi), at(q)], preferred_element_type=f32)
            total = added(total, term)
        return total

    def mirror(target, p, q, block):
        rounded = block.astype(bf16)
        target[at(p), at(q)] = rounded
        if p != q:
            target[at(q), at(p)] = rounded.T

    def place(i, j):
        return ORDER.index(i), ORDER.index(j)

    for n, (i, j) in enumerate(PAIRS):
        if (i, j) in LATE_PAIRS:
            x0[n] = halo.block(i, j, turned[TURNED.index((i, j))] if (i, j) in TURNED else None)
    largest = None
    for i in range(SLOTS):
        total = halo.sums(i)
        if i in EARLY:
            total = added(sums[:, i : i + 1], total) if total is not None else sums[:, i : i + 1]
        top = jnp.max(total, axis=0, keepdims=True)
        largest = top if largest is None else jnp.maximum(largest, top)
    inv = 1.0 / (2.0 * jnp.sqrt(largest + 1e-06))

    for n, (i, j) in enumerate(PAIRS):
        block = early[EARLY_PAIRS.index((i, j))] if (i, j) in EARLY_PAIRS else x0[n]
        x0[n] = block * inv
        mirror(x0b, *place(i, j), x0[n])
    upper = [(p, q) for p in range(SLOTS) for q in range(p, SLOTS)]
    for p, q in upper:
        mirror(q0b, p, q, product(x0b, x0b, p, q))
    for p, q in upper:
        block = -0.5 * product(x0b, q0b, p, q)
        if coupled(p, q):
            block = 1.5 * x0[PAIRS.index((ORDER[p], ORDER[q]))] + block
        if p == 0:
            first[:, at(q)] = block
        mirror(x1b, p, q, block)
    for q in range(SLOTS):
        y[:, at(q)] = product(x1b, x1b, 0, q).astype(bf16)
    sign = 1.5 * first[:, at(0)] - 0.5 * jnp.dot(y[...], x1b[:, at(0)], preferred_element_type=f32)
    result = 0.5 * jnp.where(eye, 1.0 + sign, sign)
    core[...] = result
    occupied = jnp.sum(jnp.where(eye, result, 0.0), axis=1, keepdims=True)
    lanes = charges.shape[1]
    atoms = blk // ORBS
    atom = lax.broadcasted_iota(jnp.int32, (blk, lanes), 0) // ORBS + slots[0, 0] % 2 * atoms
    lane = lax.broadcasted_iota(jnp.int32, (blk, lanes), 1)
    charges[...] = jnp.sum(
        jnp.where(atom == lane, 4.0 / ORBS - 2.0 * occupied, 0.0), axis=0, keepdims=True
    )


def rest_kernel(core, first, y, x1b, density, out, sems):
    blk = core.shape[0]

    def write(q, block):
        out[q] = block
        copy = pltpu.make_async_copy(
            out.at[q], density.at[0, :, pl.ds(ORDER[q] * blk, blk)], sems.at[q]
        )
        copy.start()
        return copy

    copies = [write(0, core[...])]
    for q in range(1, SLOTS):
        at = slice(q * blk, (q + 1) * blk)
        product = jnp.dot(y[...], x1b[:, at], preferred_element_type=jnp.float32)
        copies.append(write(q, 0.75 * first[:, at] - 0.25 * product))
    for copy in copies:
        copy.wait()


VMEM = pl.BlockSpec(memory_space=pltpu.VMEM)
SMEM = pl.BlockSpec(memory_space=pltpu.SMEM)
ANY = pl.BlockSpec(memory_space=pl.ANY)


SMALL = pl.CostEstimate(flops=1, bytes_accessed=1, transcendentals=0)


LIMIT = pltpu.CompilerParams(vmem_limit_bytes=20 * MIB)


def early_part(slots, potential, own, *halves):
    blk = own.shape[-1]
    return pl.pallas_call(
        early_kernel,
        out_shape=(
            jax.ShapeDtypeStruct((len(EARLY_PAIRS), blk, blk), jnp.float32),
            jax.ShapeDtypeStruct((len(TURNED), blk, blk), own.dtype),
            jax.ShapeDtypeStruct((blk, LANES), jnp.float32),
        ),
        in_specs=[SMEM, SMEM] + [VMEM] * 5,
        out_specs=(VMEM, VMEM, VMEM),
        compiler_params=LIMIT,
        cost_estimate=SMALL,
        name="early_blocks",
    )(slots, potential, own, *halves)


def late_part(slots, potential, own, early, turned, sums, r4, r3):
    blk = own.shape[-1]
    order = SLOTS * blk
    return pl.pallas_call(
        late_kernel,
        out_shape=(
            jax.ShapeDtypeStruct((1, LANES), jnp.float32),
            jax.ShapeDtypeStruct((blk, blk), jnp.float32),
            jax.ShapeDtypeStruct((blk, order), jnp.float32),
            jax.ShapeDtypeStruct((blk, order), jnp.bfloat16),
            jax.ShapeDtypeStruct((order, order), jnp.bfloat16),
        ),
        in_specs=[SMEM, SMEM] + [VMEM] * 6,
        out_specs=(VMEM,) * 5,
        scratch_shapes=[
            pltpu.VMEM((len(PAIRS), blk, blk), jnp.float32),
            pltpu.VMEM((order, order), jnp.bfloat16),
            pltpu.VMEM((order, order), jnp.bfloat16),
        ],
        compiler_params=LIMIT,
        name="core_charges",
    )(slots, potential, own, early, turned, sums, r4, r3)


def rest_part(core, first, y, x1b):
    blk, order = first.shape
    return pl.pallas_call(
        rest_kernel,
        out_shape=jax.ShapeDtypeStruct((1, blk, order), jnp.float32),
        in_specs=[VMEM] * 4,
        out_specs=ANY,
        scratch_shapes=[
            pltpu.VMEM((SLOTS, blk, blk), jnp.float32),
            pltpu.SemaphoreType.DMA((SLOTS,)),
        ],
        compiler_params=LIMIT,
        cost_estimate=pl.CostEstimate(
            flops=2 * blk * order * order, bytes_accessed=4 * blk * order, transcendentals=0
        ),
        name="density_rows",
    )(core, first, y, x1b)


def pack_kernel(groups, own, earlier, *packs):
    for group, pack in zip(groups, packs):
        for index, k in enumerate(group):
            pack[0, index] = own[0, k]


def packed(own, earlier, *groups):
    blk = own.shape[-1]
    return pl.pallas_call(
        functools.partial(pack_kernel, groups),
        out_shape=tuple(
            jax.ShapeDtypeStruct((1, len(group), blk, blk), own.dtype) for group in groups
        ),
        in_specs=[VMEM, ANY],
        out_specs=(VMEM,) * len(groups),
        compiler_params=LIMIT,
        cost_estimate=SMALL,
        name="pack_halo",
    )(own, earlier)


def order_kernel(slots, *refs):
    blocks, out = refs[:-1], refs[-1]
    me = slots[0, 0] // 2
    height = blocks[0].shape[0]
    for dy, block in enumerate(blocks):
        for row in range(height):
            dx, dz, dcore = row // 8, row // 2 % 4, row % 2
            target = me ^ (((dy * 4 + dx) * 2 + dcore) * 4 + dz)
            out[pl.ds(target, 1), :] = block[row : row + 1, :]


def in_order(slots, blocks):
    height, lanes = blocks[0].shape
    return pl.pallas_call(
        order_kernel,
        out_shape=jax.ShapeDtypeStruct((len(blocks) * height, lanes), blocks[0].dtype),
        in_specs=[SMEM] + [VMEM] * len(blocks),
        out_specs=VMEM,
        compiler_params=LIMIT,
        name="order_charges",
    )(slots, *blocks)


def shards(hamiltonian, partitions, chemical_potential):
    n_dom, n_sub = lax.axis_size("dom"), lax.axis_size("sub")
    potential = chemical_potential.reshape(1, 1)

    def up(x, axis, size):
        return lax.ppermute(x, axis, [(i, (i + 1) % size) for i in range(size)])

    def down(x, axis, size):
        return lax.ppermute(x, axis, [((i + 1) % size, i) for i in range(size)])

    def swapped(x, mask):
        return lax.ppermute(x, ("dom", "sub"), [(p, p ^ mask) for p in range(n_dom * n_sub)])

    def others(x, first, second):
        return [swapped(x, mask) for mask in (first, second, first + second)]

    sub_down, sub_up = packed(hamiltonian, hamiltonian, SENT[4], SENT[3])
    dom_parts = packed(
        hamiltonian, sub_down, SENT[1][:2], SENT[1][2:], SENT[2][:2], SENT[2][2:]
    )
    r4 = down(sub_down, "sub", n_sub)
    r3 = up(sub_up, "sub", n_sub)
    halves = [up(x, "dom", n_dom) for x in dom_parts[:2]]
    halves += [down(x, "dom", n_dom) for x in dom_parts[2:]]
    early, turned, sums = early_part(partitions, potential, hamiltonian, *halves)
    row, *held = late_part(
        partitions, potential, hamiltonian, early, turned, sums, r4, r3
    )
    density = rest_part(*held)
    near, core, both = others(row, 1, 8)
    block = jnp.concatenate([row + near, core + both], axis=0)
    block = jnp.concatenate([block] + others(block, 2, 4), axis=0)
    block = jnp.concatenate([block] + others(block, 16, 32), axis=0)
    charges = in_order(partitions, [block] + others(block, 64, 128)).reshape(-1)
    return (density, charges)


def solution(mesh):
    return jax.shard_map(
        shards,
        mesh=mesh,
        in_specs=(P(("dom", "sub"), None, None, None), P(("dom", "sub"), None), P()),
        out_specs=(P(("dom", "sub"), None, None), P()),
        check_vma=False,
    )
```

```python
import functools

import jax
import jax.numpy as jnp
from jax import lax
from jax.experimental import pallas as pl
from jax.experimental.pallas import tpu as pltpu
from jax.sharding import Mesh
from jax.sharding import PartitionSpec as P

ORBS = 4
SLOTS = 5
LANES = 128
MIB = 1024 * 1024
STEPS = ((0, 0), (-1, 0), (1, 0), (0, -1), (0, 1))
SENT = {1: (4, 7, 6, 8), 2: (4, 1, 0, 2), 3: (4, 5, 2, 8), 4: (4, 3, 0, 6)}
ORDER = (0, 3, 4, 1, 2)
EARLY = (0, 1, 2)


def tile_of(i, j):
    da = STEPS[j][0] - STEPS[i][0]
    db = STEPS[j][1] - STEPS[i][1]
    if abs(da) > 1 or abs(db) > 1:
        return None
    return (da + 1) * 3 + db + 1


PAIRS = [
    (ORDER[p], ORDER[q])
    for p in range(SLOTS)
    for q in range(p, SLOTS)
    if tile_of(ORDER[p], ORDER[q]) is not None
]
EARLY_PAIRS = [pair for pair in PAIRS if pair[0] in EARLY and pair[1] in EARLY]
LATE_PAIRS = [pair for pair in PAIRS if pair not in EARLY_PAIRS]
TURNED = [(i, j) for i, j in LATE_PAIRS if j in EARLY]


def runs(blocks):
    found = []
    for k in blocks:
        if found and found[-1][1] == k:
            found[-1][1] = k + 1
        else:
            found.append([k, k + 1])
    return found


def added(old, new):
    return new if old is None else old + new


class Halo:
    def __init__(self, slots, potential, own, received):
        self.own, self.received = own, received
        blk = own.shape[-1]
        rows = lax.broadcasted_iota(jnp.int32, (blk, blk), 0)
        self.eye = rows == lax.broadcasted_iota(jnp.int32, (blk, blk), 1)
        self.live = [(slots[0, i] >= 0).astype(jnp.float32) for i in range(SLOTS)]
        self.potential = potential[0, 0]
        self.row_sums = [None] * SLOTS
        self.col_sums = [None] * SLOTS

    def tile(self, i, j):
        k = tile_of(i, j)
        if i == 0:
            return self.own[0, k]
        parts = self.received[i]
        place = SENT[i].index(k)
        return parts[place // parts[0].shape[1]][0, place % parts[0].shape[1]]

    def block(self, i, j, turned=None):
        if turned is None:
            turned = self.tile(j, i).T
        both = self.tile(i, j).astype(jnp.float32) + turned.astype(jnp.float32)
        if i == j:
            block = (jnp.where(self.eye, self.potential, 0.0) - 0.5 * both) * self.live[i]
        else:
            block = both * (-0.5 * self.live[i] * self.live[j])
        squares = block * block
        folded = squares[:, :LANES]
        for lane in range(LANES, squares.shape[1], LANES):
            folded = folded + squares[:, lane : lane + LANES]
        self.row_sums[i] = added(self.row_sums[i], folded)
        if i != j:
            self.col_sums[j] = added(self.col_sums[j], jnp.sum(squares, axis=0, keepdims=True))
        return block

    def sums(self, i):
        total = self.row_sums[i]
        if total is not None:
            total = jnp.sum(total, axis=1, keepdims=True)
        if self.col_sums[i] is not None:
            turned = jnp.sum(jnp.where(self.eye, self.col_sums[i], 0.0), axis=1, keepdims=True)
            total = added(total, turned)
        return total


def early_kernel(slots, potential, own, r1a, r1b, r2a, r2b, blocks, turned, sums):
    halo = Halo(slots, potential, own, {1: (r1a, r1b), 2: (r2a, r2b)})
    for place, (i, j) in enumerate(TURNED):
        turned[place] = halo.tile(j, i).T
    for place, (i, j) in enumerate(EARLY_PAIRS):
        blocks[place] = halo.block(i, j)
    lane = lax.broadcasted_iota(jnp.int32, sums.shape, 1)
    total = jnp.zeros(sums.shape, jnp.float32)
    for i in EARLY:
        total = jnp.where(lane == i, halo.sums(i), total)
    sums[...] = total


def late_kernel(
    n_sub, slots, potential, own, early, turned, sums, r4, r3, density, charges,
    first, x1b, x0, x0b, q0b, out, sems,
):
    blk = own.shape[-1]
    f32, bf16 = jnp.float32, jnp.bfloat16
    halo = Halo(slots, potential, own, {3: (r3,), 4: (r4,)})
    eye = halo.eye

    def at(p, q=None):
        return slice(p * blk, (p + 1 if q is None else q) * blk)

    def coupled(p, q):
        return tile_of(ORDER[p], ORDER[q]) is not None

    def product(left, right, p, q):
        inner = [k for k in range(SLOTS) if right is not x0b or coupled(k, q)]
        total = None
        for lo, hi in runs(inner):
            term = jnp.dot(left[at(0, p + 1), at(lo, hi)], right[at(lo, hi), at(q)], preferred_element_type=f32)
            total = added(total, term)
        return total

    def mirror(target, p, q, block):
        rounded = block.astype(bf16)
        target[at(p), at(q)] = rounded
        if p != q:
            target[at(q), at(p)] = rounded.T

    def place(i, j):
        return ORDER.index(i), ORDER.index(j)

    for n, (i, j) in enumerate(PAIRS):
        if (i, j) in LATE_PAIRS:
            x0[n] = halo.block(i, j, turned[TURNED.index((i, j))] if (i, j) in TURNED else None)
    largest = None
    for i in range(SLOTS):
        total = halo.sums(i)
        if i in EARLY:
            total = added(sums[:, i : i + 1], total) if total is not None else sums[:, i : i + 1]
        top = jnp.max(total, axis=0, keepdims=True)
        largest = top if largest is None else jnp.maximum(largest, top)
    inv = 1.0 / (2.0 * jnp.sqrt(largest + 1e-06))

    for n, (i, j) in enumerate(PAIRS):
        block = early[EARLY_PAIRS.index((i, j))] if (i, j) in EARLY_PAIRS else x0[n]
        x0[n] = block * inv
        mirror(x0b, *place(i, j), x0[n])
    for p in range(SLOTS):
        for q in range(SLOTS):
            if not coupled(p, q):
                x0b[at(p), at(q)] = jnp.zeros((blk, blk), bf16)
    for q in range(SLOTS):
        panel = product(x0b, x0b, q, q)
        for p in range(q + 1):
            mirror(q0b, p, q, panel[at(p)])
    for q in range(SLOTS):
        panel = product(x0b, q0b, q, q)
        for p in range(q + 1):
            block = -0.5 * panel[at(p)]
            if coupled(p, q):
                block = 1.5 * x0[PAIRS.index((ORDER[p], ORDER[q]))] + block
            if p == 0:
                first[:, at(q)] = block
            mirror(x1b, p, q, block)
    left = jnp.concatenate(
        [product(x1b, x1b, 0, q).astype(bf16) for q in range(SLOTS)], axis=1
    )
    copies = []
    for q in range(SLOTS):
        sign = 1.5 * first[:, at(q)] - 0.5 * jnp.dot(
            left, x1b[:, at(q)], preferred_element_type=f32
        )
        if q == 0:
            sign = jnp.where(eye, 1.0 + sign, sign)
        result = 0.5 * sign
        out[q] = result
        copy = pltpu.make_async_copy(
            out.at[q], density.at[0, :, pl.ds(ORDER[q] * blk, blk)], sems.at[q]
        )
        copy.start()
        copies.append(copy)
        if q == 0:
            occupied = jnp.sum(jnp.where(eye, result, 0.0), axis=1, keepdims=True)
            lanes = charges.shape[1]
            atoms = blk // ORBS
            half = slots[0, 0] // n_sub % 2
            atom = lax.broadcasted_iota(jnp.int32, (blk, lanes), 0) // ORBS + half * atoms
            lane = lax.broadcasted_iota(jnp.int32, (blk, lanes), 1)
            charges[...] = jnp.sum(
                jnp.where(atom == lane, 4.0 / ORBS - 2.0 * occupied, 0.0), axis=0, keepdims=True
            )
    for copy in copies:
        copy.wait()


VMEM = pl.BlockSpec(memory_space=pltpu.VMEM)
SMEM = pl.BlockSpec(memory_space=pltpu.SMEM)
ANY = pl.BlockSpec(memory_space=pl.ANY)


SMALL = pl.CostEstimate(flops=1, bytes_accessed=1, transcendentals=0)


LIMIT = pltpu.CompilerParams(vmem_limit_bytes=20 * MIB)


def early_part(slots, potential, own, *halves):
    blk = own.shape[-1]
    return pl.pallas_call(
        early_kernel,
        out_shape=(
            jax.ShapeDtypeStruct((len(EARLY_PAIRS), blk, blk), jnp.float32),
            jax.ShapeDtypeStruct((len(TURNED), blk, blk), own.dtype),
            jax.ShapeDtypeStruct((blk, LANES), jnp.float32),
        ),
        in_specs=[SMEM, SMEM] + [VMEM] * 5,
        out_specs=(VMEM, VMEM, VMEM),
        compiler_params=LIMIT,
        cost_estimate=SMALL,
        name="early_blocks",
    )(slots, potential, own, *halves)


def late_part(slots, potential, own, early, turned, sums, r4, r3, n_sub):
    blk = own.shape[-1]
    order = SLOTS * blk
    return pl.pallas_call(
        functools.partial(late_kernel, n_sub),
        out_shape=(
            jax.ShapeDtypeStruct((1, blk, order), jnp.float32),
            jax.ShapeDtypeStruct((1, LANES), jnp.float32),
        ),
        in_specs=[SMEM, SMEM] + [VMEM] * 6,
        out_specs=(ANY, VMEM),
        scratch_shapes=[
            pltpu.VMEM((blk, order), jnp.float32),
            pltpu.VMEM((order, order), jnp.bfloat16),
            pltpu.VMEM((len(PAIRS), blk, blk), jnp.float32),
            pltpu.VMEM((order, order), jnp.bfloat16),
            pltpu.VMEM((order, order), jnp.bfloat16),
            pltpu.VMEM((SLOTS, blk, blk), jnp.float32),
            pltpu.SemaphoreType.DMA((SLOTS,)),
        ],
        compiler_params=LIMIT,
        name="density_rows",
    )(slots, potential, own, early, turned, sums, r4, r3)


def pack_kernel(groups, own, earlier, *packs):
    for group, pack in zip(groups, packs):
        for index, k in enumerate(group):
            pack[0, index] = own[0, k]


def packed(own, earlier, *groups):
    blk = own.shape[-1]
    return pl.pallas_call(
        functools.partial(pack_kernel, groups),
        out_shape=tuple(
            jax.ShapeDtypeStruct((1, len(group), blk, blk), own.dtype) for group in groups
        ),
        in_specs=[VMEM, ANY],
        out_specs=(VMEM,) * len(groups),
        compiler_params=LIMIT,
        cost_estimate=SMALL,
        name="pack_halo",
    )(own, earlier)


def order_kernel(rows, out):
    half = rows.shape[0] // 2
    even = rows[pl.ds(0, half, stride=2), :]
    odd = rows[pl.ds(1, half, stride=2), :]
    low = lax.broadcasted_iota(jnp.int32, even.shape, 1) < LANES // 2
    first = jnp.where(low, even, pltpu.roll(odd, LANES // 2, 1))
    second = jnp.where(low, pltpu.roll(even, LANES // 2, 1), odd)
    for chip in range(half // 4):
        out[8 * chip : 8 * chip + 4, :] = first[4 * chip : 4 * chip + 4]
        out[8 * chip + 4 : 8 * chip + 8, :] = second[4 * chip : 4 * chip + 4]


def in_order(rows):
    return pl.pallas_call(
        order_kernel,
        out_shape=jax.ShapeDtypeStruct(rows.shape, rows.dtype),
        in_specs=[VMEM],
        out_specs=VMEM,
        compiler_params=LIMIT,
        name="order_charges",
    )(rows)


def shards(hamiltonian, partitions, chemical_potential):
    n_chip, n_core = lax.axis_size("chip"), lax.axis_size("core")
    n_dom, n_sub = n_chip * n_core, lax.axis_size("sub")
    dom = ("chip", "core")
    potential = chemical_potential.reshape(1, 1)

    def up(x, axis, size):
        return lax.ppermute(x, axis, [(i, (i + 1) % size) for i in range(size)])

    def down(x, axis, size):
        return lax.ppermute(x, axis, [((i + 1) % size, i) for i in range(size)])

    def joined(tiles):
        return jnp.concatenate([hamiltonian[:, k : k + 1] for k in tiles], axis=1)

    sub_up, sub_down = joined(SENT[3]), joined(SENT[4])
    dom_parts = packed(
        hamiltonian, sub_up, SENT[1][:2], SENT[1][2:], SENT[2][:2], SENT[2][2:]
    )
    r4 = down(sub_down, "sub", n_sub)
    r3 = up(sub_up, "sub", n_sub)
    halves = [up(x, dom, n_dom) for x in dom_parts[:2]]
    halves += [down(x, dom, n_dom) for x in dom_parts[2:]]
    early, turned, sums = early_part(partitions, potential, hamiltonian, *halves)
    density, row = late_part(
        partitions, potential, hamiltonian, early, turned, sums, r4, r3, n_sub
    )
    row = row + lax.ppermute(row, "core", [(i, n_core - 1 - i) for i in range(n_core)])
    copies = jnp.broadcast_to(row, (n_chip * n_sub, LANES))
    rows = lax.all_to_all(copies, ("chip", "sub"), 0, 0, tiled=True)
    return (density, in_order(rows).reshape(-1))


def solution(mesh):
    n_dom, n_sub = mesh.shape["dom"], mesh.shape["sub"]
    devices = ("chip", "core", "sub")
    cores = Mesh(mesh.devices.reshape(n_dom // 2, 2, n_sub), devices)
    return jax.shard_map(
        shards,
        mesh=cores,
        in_specs=(P(devices, None, None, None), P(devices, None), P()),
        out_specs=(P(devices, None, None), P()),
        check_vma=False,
    )
```

```python
import functools

import jax
import jax.numpy as jnp
from jax import lax
from jax.experimental import pallas as pl
from jax.experimental.pallas import tpu as pltpu
from jax.sharding import PartitionSpec as P

ORBS = 4
SLOTS = 5
LANES = 128
MIB = 1024 * 1024
STEPS = ((0, 0), (-1, 0), (1, 0), (0, -1), (0, 1))
SENT = {
    1: ((4, 7), (6, 8)),
    2: ((4, 1), (0, 2)),
    3: ((4, 5, 2, 8),),
    4: ((4, 3, 0, 6),),
}
ORDER = (0, 3, 4, 1, 2)
EARLY = (0, 1, 2)


def tile_of(i, j):
    da = STEPS[j][0] - STEPS[i][0]
    db = STEPS[j][1] - STEPS[i][1]
    if abs(da) > 1 or abs(db) > 1:
        return None
    return (da + 1) * 3 + db + 1


PAIRS = [
    (ORDER[p], ORDER[q])
    for p in range(SLOTS)
    for q in range(p, SLOTS)
    if tile_of(ORDER[p], ORDER[q]) is not None
]
EARLY_PAIRS = [pair for pair in PAIRS if pair[0] in EARLY and pair[1] in EARLY]
LATE_PAIRS = [pair for pair in PAIRS if pair not in EARLY_PAIRS]
TURNED = [(i, j) for i, j in LATE_PAIRS if j in EARLY]


def runs(blocks):
    found = []
    for k in blocks:
        if found and found[-1][1] == k:
            found[-1][1] = k + 1
        else:
            found.append([k, k + 1])
    return found


def added(old, new):
    return new if old is None else old + new


class Halo:
    def __init__(self, slots, potential, own, received):
        self.own, self.received = own, received
        blk = own.shape[-1]
        rows = lax.broadcasted_iota(jnp.int32, (blk, blk), 0)
        self.eye = rows == lax.broadcasted_iota(jnp.int32, (blk, blk), 1)
        self.live = [(slots[0, i] >= 0).astype(jnp.float32) for i in range(SLOTS)]
        self.potential = potential[0, 0]
        self.row_sums = [None] * SLOTS
        self.col_sums = [None] * SLOTS

    def tile(self, i, j):
        k = tile_of(i, j)
        if i == 0:
            return self.own[0, k]
        for part, group in zip(self.received[i], SENT[i]):
            if k in group:
                return part[0, group.index(k)]

    def block(self, i, j, turned=None):
        if turned is None:
            turned = self.tile(j, i).T
        both = self.tile(i, j).astype(jnp.float32) + turned.astype(jnp.float32)
        if i == j:
            block = (jnp.where(self.eye, self.potential, 0.0) - 0.5 * both) * self.live[i]
        else:
            block = both * (-0.5 * self.live[i] * self.live[j])
        squares = block * block
        folded = squares[:, :LANES]
        for lane in range(LANES, squares.shape[1], LANES):
            folded = folded + squares[:, lane : lane + LANES]
        self.row_sums[i] = added(self.row_sums[i], folded)
        if i != j:
            self.col_sums[j] = added(self.col_sums[j], jnp.sum(squares, axis=0, keepdims=True))
        return block

    def sums(self, i):
        total = self.row_sums[i]
        if total is not None:
            total = jnp.sum(total, axis=1, keepdims=True)
        if self.col_sums[i] is not None:
            turned = jnp.sum(jnp.where(self.eye, self.col_sums[i], 0.0), axis=1, keepdims=True)
            total = added(total, turned)
        return total


def early_kernel(slots, potential, own, r1a, r1b, r2a, r2b, blocks, turned, sums):
    halo = Halo(slots, potential, own, {1: (r1a, r1b), 2: (r2a, r2b)})
    for place, (i, j) in enumerate(TURNED):
        turned[place] = halo.tile(j, i).T
    for place, (i, j) in enumerate(EARLY_PAIRS):
        blocks[place] = halo.block(i, j)
    lane = lax.broadcasted_iota(jnp.int32, sums.shape, 1)
    total = jnp.zeros(sums.shape, jnp.float32)
    for i in EARLY:
        total = jnp.where(lane == i, halo.sums(i), total)
    sums[...] = total


def late_kernel(
    slots, potential, own, early, turned, sums, r3, r4, density, charges,
    first, y, x1b, x0, x0b, q0b, out, sems,
):
    blk = own.shape[-1]
    f32, bf16 = jnp.float32, jnp.bfloat16
    halo = Halo(slots, potential, own, {3: (r3,), 4: (r4,)})
    eye = halo.eye

    def at(p, q=None):
        return slice(p * blk, (p + 1 if q is None else q) * blk)

    def coupled(p, q):
        return tile_of(ORDER[p], ORDER[q]) is not None

    def product(left, right, p, q):
        total = None
        full = right is x0b
        inner = [
            k for k in range(SLOTS)
            if (left is not x0b or coupled(p, k)) and (not full or coupled(k, q))
        ]
        for lo, hi in runs([k for k in inner if full or k <= q]):
            term = jnp.dot(left[at(p), at(lo, hi)], right[at(lo, hi), at(q)], preferred_element_type=f32)
            total = added(total, term)
        for lo, hi in runs([k for k in inner if not full and k > q]):
            term = lax.dot_general(
                left[at(p), at(lo, hi)], right[at(q), at(lo, hi)],
                (((1,), (1,)), ((), ())), preferred_element_type=f32,
            )
            total = added(total, term)
        return total

    def mirror(target, p, q, block):
        rounded = block.astype(bf16)
        target[at(p), at(q)] = rounded
        if p != q:
            target[at(q), at(p)] = rounded.T

    def place(i, j):
        return ORDER.index(i), ORDER.index(j)

    for n, (i, j) in enumerate(LATE_PAIRS):
        x0[n] = halo.block(i, j, turned[TURNED.index((i, j))] if (i, j) in TURNED else None)
    largest = None
    for i in range(SLOTS):
        total = halo.sums(i)
        if i in EARLY:
            total = added(sums[:, i : i + 1], total) if total is not None else sums[:, i : i + 1]
        top = jnp.max(total, axis=0, keepdims=True)
        largest = top if largest is None else jnp.maximum(largest, top)
    inv = 1.0 / (2.0 * jnp.sqrt(largest + 1e-06))

    def unscaled(i, j):
        if (i, j) in EARLY_PAIRS:
            return early[EARLY_PAIRS.index((i, j))]
        return x0[LATE_PAIRS.index((i, j))]

    for i, j in PAIRS:
        mirror(x0b, *place(i, j), unscaled(i, j) * inv)
    linear = 1.5 * inv
    upper = [(p, q) for p in range(SLOTS) for q in range(p, SLOTS)]
    for p, q in upper:
        q0b[at(p), at(q)] = product(x0b, x0b, p, q).astype(bf16)
    for p, q in upper:
        block = -0.5 * product(x0b, q0b, p, q)
        if coupled(p, q):
            block = linear * unscaled(ORDER[p], ORDER[q]) + block
        if p == 0:
            first[:, at(q)] = block
        x1b[at(p), at(q)] = block.astype(bf16)
    for q in range(SLOTS):
        y[:, at(q)] = product(x1b, x1b, 0, q).astype(bf16)
    copies = []
    for q in range(SLOTS):
        sign = 1.5 * first[:, at(q)] - 0.5 * product(y, x1b, 0, q)
        if q == 0:
            sign = jnp.where(eye, 1.0 + sign, sign)
        result = 0.5 * sign
        out[q] = result
        copy = pltpu.make_async_copy(
            out.at[q], density.at[0, :, pl.ds(ORDER[q] * blk, blk)], sems.at[q]
        )
        copy.start()
        copies.append(copy)
        if q == 0:
            occupied = jnp.sum(jnp.where(eye, result, 0.0), axis=1, keepdims=True)
            lanes = charges.shape[1]
            atoms = blk // ORBS
            half = slots[0, 0] % 2
            atom = lax.broadcasted_iota(jnp.int32, (blk, lanes), 0) // ORBS + half * atoms
            lane = lax.broadcasted_iota(jnp.int32, (blk, lanes), 1)
            charges[...] = jnp.sum(
                jnp.where(atom == lane, 4.0 / ORBS - 2.0 * occupied, 0.0), axis=0, keepdims=True
            )
    for copy in copies:
        copy.wait()


VMEM = pl.BlockSpec(memory_space=pltpu.VMEM)
SMEM = pl.BlockSpec(memory_space=pltpu.SMEM)
ANY = pl.BlockSpec(memory_space=pl.ANY)


SMALL = pl.CostEstimate(flops=1, bytes_accessed=1, transcendentals=0)


LIMIT = pltpu.CompilerParams(vmem_limit_bytes=20 * MIB)


def early_part(slots, potential, own, *halves):
    blk = own.shape[-1]
    return pl.pallas_call(
        early_kernel,
        out_shape=(
            jax.ShapeDtypeStruct((len(EARLY_PAIRS), blk, blk), jnp.float32),
            jax.ShapeDtypeStruct((len(TURNED), blk, blk), own.dtype),
            jax.ShapeDtypeStruct((blk, LANES), jnp.float32),
        ),
        in_specs=[SMEM, SMEM] + [VMEM] * 5,
        out_specs=(VMEM, VMEM, VMEM),
        compiler_params=LIMIT,
        cost_estimate=SMALL,
        name="early_blocks",
    )(slots, potential, own, *halves)


def late_part(slots, potential, own, early, turned, sums, r3, r4):
    blk = own.shape[-1]
    order = SLOTS * blk
    return pl.pallas_call(
        late_kernel,
        out_shape=(
            jax.ShapeDtypeStruct((1, blk, order), jnp.float32),
            jax.ShapeDtypeStruct((1, LANES), jnp.float32),
        ),
        in_specs=[SMEM, SMEM] + [VMEM] * 6,
        out_specs=(ANY, VMEM),
        scratch_shapes=[
            pltpu.VMEM((blk, order), jnp.float32),
            pltpu.VMEM((blk, order), jnp.bfloat16),
            pltpu.VMEM((order, order), jnp.bfloat16),
            pltpu.VMEM((len(LATE_PAIRS), blk, blk), jnp.float32),
            pltpu.VMEM((order, order), jnp.bfloat16),
            pltpu.VMEM((order, order), jnp.bfloat16),
            pltpu.VMEM((SLOTS, blk, blk), jnp.float32),
            pltpu.SemaphoreType.DMA((SLOTS,)),
        ],
        compiler_params=LIMIT,
        name="density_rows",
    )(slots, potential, own, early, turned, sums, r3, r4)


def pack_kernel(groups, own, earlier, *packs):
    for group, pack in zip(groups, packs):
        for index, k in enumerate(group):
            pack[0, index] = own[0, k]


def packed(own, earlier, *groups):
    blk = own.shape[-1]
    return pl.pallas_call(
        functools.partial(pack_kernel, groups),
        out_shape=tuple(
            jax.ShapeDtypeStruct((1, len(group), blk, blk), own.dtype) for group in groups
        ),
        in_specs=[VMEM, ANY],
        out_specs=(VMEM,) * len(groups),
        compiler_params=LIMIT,
        cost_estimate=SMALL,
        name="pack_halo",
    )(own, earlier)


def pair_kernel(rows, out):
    half = out.shape[0]
    out[...] = rows[pl.ds(0, half, stride=2), :] + rows[pl.ds(1, half, stride=2), :]


def paired(rows):
    return pl.pallas_call(
        pair_kernel,
        out_shape=jax.ShapeDtypeStruct((rows.shape[0] // 2, rows.shape[1]), rows.dtype),
        in_specs=[VMEM],
        out_specs=VMEM,
        compiler_params=LIMIT,
        name="pair_charges",
    )(rows)


def shards(hamiltonian, partitions, chemical_potential):
    n_dom, n_sub = lax.axis_size("dom"), lax.axis_size("sub")
    potential = chemical_potential.reshape(1, 1)

    def up(x, axis, size):
        return lax.ppermute(x, axis, [(i, (i + 1) % size) for i in range(size)])

    def down(x, axis, size):
        return lax.ppermute(x, axis, [((i + 1) % size, i) for i in range(size)])

    sub_down, sub_up = packed(hamiltonian, hamiltonian, *SENT[4], *SENT[3])
    dom_parts = packed(hamiltonian, sub_down, *SENT[1], *SENT[2])
    r4 = down(sub_down, "sub", n_sub)
    r3 = up(sub_up, "sub", n_sub)
    halves = [up(x, "dom", n_dom) for x in dom_parts[:2]]
    halves += [down(x, "dom", n_dom) for x in dom_parts[2:]]
    early, turned, sums = early_part(partitions, potential, hamiltonian, *halves)
    density, row = late_part(
        partitions, potential, hamiltonian, early, turned, sums, r3, r4
    )
    copies = jnp.broadcast_to(row, (n_dom * n_sub, LANES))
    rows = lax.all_to_all(copies, ("dom", "sub"), 0, 0, tiled=True)
    return (density, paired(rows).reshape(-1))


def solution(mesh):
    return jax.shard_map(
        shards,
        mesh=mesh,
        in_specs=(P(("dom", "sub"), None, None, None), P(("dom", "sub"), None), P()),
        out_specs=(P(("dom", "sub"), None, None), P()),
        check_vma=False,
    )
```

```python
import functools

import jax
import jax.numpy as jnp
from jax import lax
from jax.experimental import pallas as pl
from jax.experimental.pallas import tpu as pltpu
from jax.sharding import PartitionSpec as P

ORBS = 4
SLOTS = 5
LANES = 128
MIB = 1024 * 1024
STEPS = ((0, 0), (-1, 0), (1, 0), (0, -1), (0, 1))
SENT = {
    1: ((4, 7), (6, 8)),
    2: ((4, 1), (0, 2)),
    3: ((4, 5, 2, 8),),
    4: ((4, 3, 0, 6),),
}
ORDER = (0, 3, 4, 1, 2)
EARLY = (0, 1, 2)


def tile_of(i, j):
    da = STEPS[j][0] - STEPS[i][0]
    db = STEPS[j][1] - STEPS[i][1]
    if abs(da) > 1 or abs(db) > 1:
        return None
    return (da + 1) * 3 + db + 1


PAIRS = [
    (ORDER[p], ORDER[q])
    for p in range(SLOTS)
    for q in range(p, SLOTS)
    if tile_of(ORDER[p], ORDER[q]) is not None
]
EARLY_PAIRS = [pair for pair in PAIRS if pair[0] in EARLY and pair[1] in EARLY]
LATE_PAIRS = [pair for pair in PAIRS if pair not in EARLY_PAIRS]
TURNED = [(i, j) for i, j in LATE_PAIRS if j in EARLY]


def runs(blocks):
    found = []
    for k in blocks:
        if found and found[-1][1] == k:
            found[-1][1] = k + 1
        else:
            found.append([k, k + 1])
    return found


def added(old, new):
    return new if old is None else old + new


class Halo:
    def __init__(self, slots, potential, own, received):
        self.own, self.received = own, received
        blk = own.shape[-1]
        rows = lax.broadcasted_iota(jnp.int32, (blk, blk), 0)
        self.eye = rows == lax.broadcasted_iota(jnp.int32, (blk, blk), 1)
        self.live = [(slots[0, i] >= 0).astype(jnp.float32) for i in range(SLOTS)]
        self.potential = potential[0, 0]
        self.row_sums = [None] * SLOTS
        self.col_sums = [None] * SLOTS

    def tile(self, i, j):
        k = tile_of(i, j)
        if i == 0:
            return self.own[0, k]
        for part, group in zip(self.received[i], SENT[i]):
            if k in group:
                return part[0, group.index(k)]

    def block(self, i, j, turned=None):
        if turned is None:
            turned = self.tile(j, i).T
        both = self.tile(i, j).astype(jnp.float32) + turned.astype(jnp.float32)
        if i == j:
            block = (jnp.where(self.eye, self.potential, 0.0) - 0.5 * both) * self.live[i]
        else:
            block = both * (-0.5 * self.live[i] * self.live[j])
        squares = block * block
        folded = squares[:, :LANES]
        for lane in range(LANES, squares.shape[1], LANES):
            folded = folded + squares[:, lane : lane + LANES]
        self.row_sums[i] = added(self.row_sums[i], folded)
        if i != j:
            self.col_sums[j] = added(self.col_sums[j], jnp.sum(squares, axis=0, keepdims=True))
        return block

    def sums(self, i):
        total = self.row_sums[i]
        if total is not None:
            total = jnp.sum(total, axis=1, keepdims=True)
        if self.col_sums[i] is not None:
            turned = jnp.sum(jnp.where(self.eye, self.col_sums[i], 0.0), axis=1, keepdims=True)
            total = added(total, turned)
        return total


def early_kernel(slots, potential, own, r1a, r1b, r2a, r2b, blocks, turned, sums):
    halo = Halo(slots, potential, own, {1: (r1a, r1b), 2: (r2a, r2b)})
    for place, (i, j) in enumerate(TURNED):
        turned[place] = halo.tile(j, i).T
    for place, (i, j) in enumerate(EARLY_PAIRS):
        blocks[place] = halo.block(i, j)
    lane = lax.broadcasted_iota(jnp.int32, sums.shape, 1)
    total = jnp.zeros(sums.shape, jnp.float32)
    for i in EARLY:
        total = jnp.where(lane == i, halo.sums(i), total)
    sums[...] = total


def late_kernel(
    slots, potential, own, early, turned, sums, r3, r4, density, charges,
    first, y, x1b, x0, x0b, q0b, out, sems,
):
    blk = own.shape[-1]
    f32, bf16 = jnp.float32, jnp.bfloat16
    halo = Halo(slots, potential, own, {3: (r3,), 4: (r4,)})
    eye = halo.eye

    def at(p, q=None):
        return slice(p * blk, (p + 1 if q is None else q) * blk)

    def coupled(p, q):
        return tile_of(ORDER[p], ORDER[q]) is not None

    def product(left, right, p, q):
        total = None
        full = right is x0b
        inner = [
            k for k in range(SLOTS)
            if (left is not x0b or coupled(p, k)) and (not full or coupled(k, q))
        ]
        for lo, hi in runs([k for k in inner if full or k <= q]):
            term = jnp.dot(left[at(p), at(lo, hi)], right[at(lo, hi), at(q)], preferred_element_type=f32)
            total = added(total, term)
        for lo, hi in runs([k for k in inner if not full and k > q]):
            term = lax.dot_general(
                left[at(p), at(lo, hi)], right[at(q), at(lo, hi)],
                (((1,), (1,)), ((), ())), preferred_element_type=f32,
            )
            total = added(total, term)
        return total

    def mirror(target, p, q, block):
        rounded = block.astype(bf16)
        target[at(p), at(q)] = rounded
        if p != q:
            target[at(q), at(p)] = rounded.T

    def place(i, j):
        return ORDER.index(i), ORDER.index(j)

    for n, (i, j) in enumerate(LATE_PAIRS):
        x0[n] = halo.block(i, j, turned[TURNED.index((i, j))] if (i, j) in TURNED else None)
    largest = None
    for i in range(SLOTS):
        total = halo.sums(i)
        if i in EARLY:
            total = added(sums[:, i : i + 1], total) if total is not None else sums[:, i : i + 1]
        top = jnp.max(total, axis=0, keepdims=True)
        largest = top if largest is None else jnp.maximum(largest, top)
    inv = 1.0 / (2.0 * jnp.sqrt(largest + 1e-06))

    def unscaled(i, j):
        if (i, j) in EARLY_PAIRS:
            return early[EARLY_PAIRS.index((i, j))]
        return x0[LATE_PAIRS.index((i, j))]

    for i, j in PAIRS:
        mirror(x0b, *place(i, j), unscaled(i, j) * inv)
    linear = 1.5 * inv
    upper = [(p, q) for p in range(SLOTS) for q in range(p, SLOTS)]
    for p, q in upper:
        q0b[at(p), at(q)] = product(x0b, x0b, p, q).astype(bf16)
    for p, q in upper:
        block = -0.5 * product(x0b, q0b, p, q)
        if coupled(p, q):
            block = linear * unscaled(ORDER[p], ORDER[q]) + block
        if p == 0:
            first[:, at(q)] = block
        x1b[at(p), at(q)] = block.astype(bf16)
    for q in range(SLOTS):
        y[:, at(q)] = product(x1b, x1b, 0, q).astype(bf16)
    copies = []
    for q in range(SLOTS):
        sign = 1.5 * first[:, at(q)] - 0.5 * product(y, x1b, 0, q)
        if q == 0:
            sign = jnp.where(eye, 1.0 + sign, sign)
        result = 0.5 * sign
        out[q] = result
        copy = pltpu.make_async_copy(
            out.at[q], density.at[0, :, pl.ds(ORDER[q] * blk, blk)], sems.at[q]
        )
        copy.start()
        copies.append(copy)
        if q == 0:
            occupied = jnp.sum(jnp.where(eye, result, 0.0), axis=1, keepdims=True)
            lanes = charges.shape[1]
            atoms = blk // ORBS
            half = slots[0, 0] % 2
            atom = lax.broadcasted_iota(jnp.int32, (blk, lanes), 0) // ORBS + half * atoms
            lane = lax.broadcasted_iota(jnp.int32, (blk, lanes), 1)
            charges[...] = jnp.sum(
                jnp.where(atom == lane, 4.0 / ORBS - 2.0 * occupied, 0.0), axis=0, keepdims=True
            )
    for copy in copies:
        copy.wait()


VMEM = pl.BlockSpec(memory_space=pltpu.VMEM)
SMEM = pl.BlockSpec(memory_space=pltpu.SMEM)
ANY = pl.BlockSpec(memory_space=pl.ANY)


SMALL = pl.CostEstimate(flops=1, bytes_accessed=1, transcendentals=0)


LIMIT = pltpu.CompilerParams(vmem_limit_bytes=20 * MIB)


def early_part(slots, potential, own, *halves):
    blk = own.shape[-1]
    return pl.pallas_call(
        early_kernel,
        out_shape=(
            jax.ShapeDtypeStruct((len(EARLY_PAIRS), blk, blk), jnp.float32),
            jax.ShapeDtypeStruct((len(TURNED), blk, blk), own.dtype),
            jax.ShapeDtypeStruct((blk, LANES), jnp.float32),
        ),
        in_specs=[SMEM, SMEM] + [VMEM] * 5,
        out_specs=(VMEM, VMEM, VMEM),
        compiler_params=LIMIT,
        cost_estimate=SMALL,
        name="early_blocks",
    )(slots, potential, own, *halves)


def late_part(slots, potential, own, early, turned, sums, r3, r4):
    blk = own.shape[-1]
    order = SLOTS * blk
    return pl.pallas_call(
        late_kernel,
        out_shape=(
            jax.ShapeDtypeStruct((1, blk, order), jnp.float32),
            jax.ShapeDtypeStruct((1, LANES), jnp.float32),
        ),
        in_specs=[SMEM, SMEM] + [VMEM] * 6,
        out_specs=(ANY, VMEM),
        scratch_shapes=[
            pltpu.VMEM((blk, order), jnp.float32),
            pltpu.VMEM((blk, order), jnp.bfloat16),
            pltpu.VMEM((order, order), jnp.bfloat16),
            pltpu.VMEM((len(LATE_PAIRS), blk, blk), jnp.float32),
            pltpu.VMEM((order, order), jnp.bfloat16),
            pltpu.VMEM((order, order), jnp.bfloat16),
            pltpu.VMEM((SLOTS, blk, blk), jnp.float32),
            pltpu.SemaphoreType.DMA((SLOTS,)),
        ],
        compiler_params=LIMIT,
        name="density_rows",
    )(slots, potential, own, early, turned, sums, r3, r4)


def pack_kernel(groups, own, earlier, *packs):
    for group, pack in zip(groups, packs):
        for index, k in enumerate(group):
            pack[0, index] = own[0, k]


def packed(own, earlier, *groups):
    blk = own.shape[-1]
    return pl.pallas_call(
        functools.partial(pack_kernel, groups),
        out_shape=tuple(
            jax.ShapeDtypeStruct((1, len(group), blk, blk), own.dtype) for group in groups
        ),
        in_specs=[VMEM, ANY],
        out_specs=(VMEM,) * len(groups),
        compiler_params=LIMIT,
        cost_estimate=SMALL,
        name="pack_halo",
    )(own, earlier)


def pair_kernel(rows, out):
    half = out.shape[0]
    out[...] = rows[pl.ds(0, half, stride=2), :] + rows[pl.ds(1, half, stride=2), :]


def paired(rows):
    return pl.pallas_call(
        pair_kernel,
        out_shape=jax.ShapeDtypeStruct((rows.shape[0] // 2, rows.shape[1]), rows.dtype),
        in_specs=[VMEM],
        out_specs=VMEM,
        compiler_params=LIMIT,
        name="pair_charges",
    )(rows)


def shards(hamiltonian, partitions, chemical_potential):
    n_dom, n_sub = lax.axis_size("dom"), lax.axis_size("sub")
    potential = chemical_potential.reshape(1, 1)

    def up(x, axis, size):
        return lax.ppermute(x, axis, [(i, (i + 1) % size) for i in range(size)])

    def down(x, axis, size):
        return lax.ppermute(x, axis, [((i + 1) % size, i) for i in range(size)])

    sub_down, sub_up, dom_first = packed(
        hamiltonian, hamiltonian, *SENT[4], *SENT[3], SENT[1][0]
    )
    dom_parts = packed(hamiltonian, sub_down, SENT[1][1], *SENT[2])
    r4 = down(sub_down, "sub", n_sub)
    r3 = up(sub_up, "sub", n_sub)
    halves = [up(x, "dom", n_dom) for x in (dom_first, dom_parts[0])]
    halves += [down(x, "dom", n_dom) for x in dom_parts[1:]]
    early, turned, sums = early_part(partitions, potential, hamiltonian, *halves)
    density, row = late_part(
        partitions, potential, hamiltonian, early, turned, sums, r3, r4
    )
    copies = jnp.broadcast_to(row, (n_dom * n_sub, LANES))
    rows = lax.all_to_all(copies, ("dom", "sub"), 0, 0, tiled=True)
    return (density, paired(rows).reshape(-1))


def solution(mesh):
    return jax.shard_map(
        shards,
        mesh=mesh,
        in_specs=(P(("dom", "sub"), None, None, None), P(("dom", "sub"), None), P()),
        out_specs=(P(("dom", "sub"), None, None), P()),
        check_vma=False,
    )
```

```python
import functools

import jax
import jax.numpy as jnp
from jax import lax
from jax.experimental import pallas as pl
from jax.experimental.pallas import tpu as pltpu
from jax.sharding import PartitionSpec as P

ORBS = 4
SLOTS = 5
LANES = 128
MIB = 1024 * 1024
STEPS = ((0, 0), (-1, 0), (1, 0), (0, -1), (0, 1))
SENT = {
    1: ((4, 7), (6, 8)),
    2: ((4, 1), (0, 2)),
    3: ((4, 5, 2, 8),),
    4: ((4, 3, 0, 6),),
}
ORDER = (0, 3, 4, 1, 2)
EARLY = (0, 1, 2)


def tile_of(i, j):
    da = STEPS[j][0] - STEPS[i][0]
    db = STEPS[j][1] - STEPS[i][1]
    if abs(da) > 1 or abs(db) > 1:
        return None
    return (da + 1) * 3 + db + 1


PAIRS = [
    (ORDER[p], ORDER[q])
    for p in range(SLOTS)
    for q in range(p, SLOTS)
    if tile_of(ORDER[p], ORDER[q]) is not None
]
EARLY_PAIRS = [pair for pair in PAIRS if pair[0] in EARLY and pair[1] in EARLY]
LATE_PAIRS = [pair for pair in PAIRS if pair not in EARLY_PAIRS]


def runs(blocks):
    found = []
    for k in blocks:
        if found and found[-1][1] == k:
            found[-1][1] = k + 1
        else:
            found.append([k, k + 1])
    return found


def added(old, new):
    return new if old is None else old + new


class Halo:
    def __init__(self, slots, potential, own, received):
        self.own, self.received = own, received
        blk = own.shape[-1]
        rows = lax.broadcasted_iota(jnp.int32, (blk, blk), 0)
        self.eye = rows == lax.broadcasted_iota(jnp.int32, (blk, blk), 1)
        self.live = [(slots[0, i] >= 0).astype(jnp.float32) for i in range(SLOTS)]
        self.potential = potential[0, 0]
        self.row_sums = [None] * SLOTS
        self.col_sums = [None] * SLOTS

    def tile(self, i, j):
        k = tile_of(i, j)
        if i == 0:
            return self.own[0, k]
        for part, group in zip(self.received[i], SENT[i]):
            if k in group:
                return part[0, group.index(k)]

    def block(self, i, j):
        both = self.tile(i, j).astype(jnp.float32) + self.tile(j, i).T.astype(jnp.float32)
        if i == j:
            block = (jnp.where(self.eye, self.potential, 0.0) - 0.5 * both) * self.live[i]
        else:
            block = both * (-0.5 * self.live[i] * self.live[j])
        squares = block * block
        folded = squares[:, :LANES]
        for lane in range(LANES, squares.shape[1], LANES):
            folded = folded + squares[:, lane : lane + LANES]
        self.row_sums[i] = added(self.row_sums[i], folded)
        if i != j:
            self.col_sums[j] = added(self.col_sums[j], jnp.sum(squares, axis=0, keepdims=True))
        return block

    def sums(self, i):
        total = self.row_sums[i]
        if total is not None:
            total = jnp.sum(total, axis=1, keepdims=True)
        if self.col_sums[i] is not None:
            turned = jnp.sum(jnp.where(self.eye, self.col_sums[i], 0.0), axis=1, keepdims=True)
            total = added(total, turned)
        return total


def early_kernel(slots, potential, own, r1a, r2a, blocks, sums):
    halo = Halo(slots, potential, own, {1: (r1a,), 2: (r2a,)})
    for place, (i, j) in enumerate(EARLY_PAIRS):
        blocks[place] = halo.block(i, j)
    lane = lax.broadcasted_iota(jnp.int32, sums.shape, 1)
    total = jnp.zeros(sums.shape, jnp.float32)
    for i in EARLY:
        total = jnp.where(lane == i, halo.sums(i), total)
    sums[...] = total


def late_kernel(
    slots, potential, own, early, sums, r1b, r2b, r3, r4, density, charges,
    first, y, x1b, x0, x0b, q0b, out, sems,
):
    blk = own.shape[-1]
    f32, bf16 = jnp.float32, jnp.bfloat16
    halo = Halo(slots, potential, own, {1: (None, r1b), 2: (None, r2b), 3: (r3,), 4: (r4,)})
    eye = halo.eye

    def at(p, q=None):
        return slice(p * blk, (p + 1 if q is None else q) * blk)

    def coupled(p, q):
        return tile_of(ORDER[p], ORDER[q]) is not None

    def product(left, right, p, q):
        total = None
        full = right is x0b
        inner = [
            k for k in range(SLOTS)
            if (left is not x0b or coupled(p, k)) and (not full or coupled(k, q))
        ]
        for lo, hi in runs([k for k in inner if full or k <= q]):
            term = jnp.dot(left[at(p), at(lo, hi)], right[at(lo, hi), at(q)], preferred_element_type=f32)
            total = added(total, term)
        for lo, hi in runs([k for k in inner if not full and k > q]):
            term = lax.dot_general(
                left[at(p), at(lo, hi)], right[at(q), at(lo, hi)],
                (((1,), (1,)), ((), ())), preferred_element_type=f32,
            )
            total = added(total, term)
        return total

    def mirror(target, p, q, block):
        rounded = block.astype(bf16)
        target[at(p), at(q)] = rounded
        if p != q:
            target[at(q), at(p)] = rounded.T

    def place(i, j):
        return ORDER.index(i), ORDER.index(j)

    for n, (i, j) in enumerate(LATE_PAIRS):
        x0[n] = halo.block(i, j)
    largest = None
    for i in range(SLOTS):
        total = halo.sums(i)
        if i in EARLY:
            total = added(sums[:, i : i + 1], total) if total is not None else sums[:, i : i + 1]
        top = jnp.max(total, axis=0, keepdims=True)
        largest = top if largest is None else jnp.maximum(largest, top)
    inv = 1.0 / (2.0 * jnp.sqrt(largest + 1e-06))

    def unscaled(i, j):
        if (i, j) in EARLY_PAIRS:
            return early[EARLY_PAIRS.index((i, j))]
        return x0[LATE_PAIRS.index((i, j))]

    for i, j in PAIRS:
        mirror(x0b, *place(i, j), unscaled(i, j) * inv)
    linear = 1.5 * inv
    upper = [(p, q) for p in range(SLOTS) for q in range(p, SLOTS)]
    for p, q in upper:
        q0b[at(p), at(q)] = product(x0b, x0b, p, q).astype(bf16)
    for p, q in upper:
        block = -0.5 * product(x0b, q0b, p, q)
        if coupled(p, q):
            block = linear * unscaled(ORDER[p], ORDER[q]) + block
        if p == 0:
            first[:, at(q)] = block
        x1b[at(p), at(q)] = block.astype(bf16)
    for q in range(SLOTS):
        y[:, at(q)] = product(x1b, x1b, 0, q).astype(bf16)
    copies = []
    for q in range(SLOTS):
        sign = 1.5 * first[:, at(q)] - 0.5 * product(y, x1b, 0, q)
        if q == 0:
            sign = jnp.where(eye, 1.0 + sign, sign)
        result = 0.5 * sign
        out[q] = result
        copy = pltpu.make_async_copy(
            out.at[q], density.at[0, :, pl.ds(ORDER[q] * blk, blk)], sems.at[q]
        )
        copy.start()
        copies.append(copy)
        if q == 0:
            occupied = jnp.sum(jnp.where(eye, result, 0.0), axis=1, keepdims=True)
            lanes = charges.shape[1]
            atoms = blk // ORBS
            half = slots[0, 0] % 2
            atom = lax.broadcasted_iota(jnp.int32, (blk, lanes), 0) // ORBS + half * atoms
            lane = lax.broadcasted_iota(jnp.int32, (blk, lanes), 1)
            charges[...] = jnp.sum(
                jnp.where(atom == lane, 4.0 / ORBS - 2.0 * occupied, 0.0), axis=0, keepdims=True
            )
    for copy in copies:
        copy.wait()


VMEM = pl.BlockSpec(memory_space=pltpu.VMEM)
SMEM = pl.BlockSpec(memory_space=pltpu.SMEM)
ANY = pl.BlockSpec(memory_space=pl.ANY)


SMALL = pl.CostEstimate(flops=1, bytes_accessed=1, transcendentals=0)


LIMIT = pltpu.CompilerParams(vmem_limit_bytes=20 * MIB)


def early_part(slots, potential, own, r1a, r2a):
    blk = own.shape[-1]
    return pl.pallas_call(
        early_kernel,
        out_shape=(
            jax.ShapeDtypeStruct((len(EARLY_PAIRS), blk, blk), jnp.float32),
            jax.ShapeDtypeStruct((blk, LANES), jnp.float32),
        ),
        in_specs=[SMEM, SMEM] + [VMEM] * 3,
        out_specs=(VMEM, VMEM),
        compiler_params=LIMIT,
        cost_estimate=SMALL,
        name="early_blocks",
    )(slots, potential, own, r1a, r2a)


def late_part(slots, potential, own, early, sums, r1b, r2b, r3, r4):
    blk = own.shape[-1]
    order = SLOTS * blk
    return pl.pallas_call(
        late_kernel,
        out_shape=(
            jax.ShapeDtypeStruct((1, blk, order), jnp.float32),
            jax.ShapeDtypeStruct((1, LANES), jnp.float32),
        ),
        in_specs=[SMEM, SMEM] + [VMEM] * 7,
        out_specs=(ANY, VMEM),
        scratch_shapes=[
            pltpu.VMEM((blk, order), jnp.float32),
            pltpu.VMEM((blk, order), jnp.bfloat16),
            pltpu.VMEM((order, order), jnp.bfloat16),
            pltpu.VMEM((len(LATE_PAIRS), blk, blk), jnp.float32),
            pltpu.VMEM((order, order), jnp.bfloat16),
            pltpu.VMEM((order, order), jnp.bfloat16),
            pltpu.VMEM((SLOTS, blk, blk), jnp.float32),
            pltpu.SemaphoreType.DMA((SLOTS,)),
        ],
        compiler_params=LIMIT,
        name="density_rows",
    )(slots, potential, own, early, sums, r1b, r2b, r3, r4)


def pack_kernel(groups, own, earlier, *packs):
    for group, pack in zip(groups, packs):
        for index, k in enumerate(group):
            pack[0, index] = own[0, k]


def packed(own, earlier, *groups):
    blk = own.shape[-1]
    return pl.pallas_call(
        functools.partial(pack_kernel, groups),
        out_shape=tuple(
            jax.ShapeDtypeStruct((1, len(group), blk, blk), own.dtype) for group in groups
        ),
        in_specs=[VMEM, ANY],
        out_specs=(VMEM,) * len(groups),
        compiler_params=LIMIT,
        cost_estimate=SMALL,
        name="pack_halo",
    )(own, earlier)


def pair_kernel(rows, out):
    half = out.shape[0]
    out[...] = rows[pl.ds(0, half, stride=2), :] + rows[pl.ds(1, half, stride=2), :]


def paired(rows):
    return pl.pallas_call(
        pair_kernel,
        out_shape=jax.ShapeDtypeStruct((rows.shape[0] // 2, rows.shape[1]), rows.dtype),
        in_specs=[VMEM],
        out_specs=VMEM,
        compiler_params=LIMIT,
        name="pair_charges",
    )(rows)


def shards(hamiltonian, partitions, chemical_potential):
    n_dom, n_sub = lax.axis_size("dom"), lax.axis_size("sub")
    potential = chemical_potential.reshape(1, 1)

    def up(x, axis, size):
        return lax.ppermute(x, axis, [(i, (i + 1) % size) for i in range(size)])

    def down(x, axis, size):
        return lax.ppermute(x, axis, [((i + 1) % size, i) for i in range(size)])

    sub_down, sub_up, dom_first = packed(
        hamiltonian, hamiltonian, *SENT[4], *SENT[3], SENT[1][0]
    )
    dom_parts = packed(hamiltonian, sub_down, SENT[1][1], *SENT[2])
    r4 = down(sub_down, "sub", n_sub)
    r3 = up(sub_up, "sub", n_sub)
    r1a, r1b = [up(x, "dom", n_dom) for x in (dom_first, dom_parts[0])]
    r2a, r2b = [down(x, "dom", n_dom) for x in dom_parts[1:]]
    early, sums = early_part(partitions, potential, hamiltonian, r1a, r2a)
    density, row = late_part(
        partitions, potential, hamiltonian, early, sums, r1b, r2b, r3, r4
    )
    copies = jnp.broadcast_to(row, (n_dom * n_sub, LANES))
    rows = lax.all_to_all(copies, ("dom", "sub"), 0, 0, tiled=True)
    return (density, paired(rows).reshape(-1))


def solution(mesh):
    return jax.shard_map(
        shards,
        mesh=mesh,
        in_specs=(P(("dom", "sub"), None, None, None), P(("dom", "sub"), None), P()),
        out_specs=(P(("dom", "sub"), None, None), P()),
        check_vma=False,
    )
```

```python
import functools

import jax
import jax.numpy as jnp
from jax import lax
from jax.experimental import pallas as pl
from jax.experimental.pallas import tpu as pltpu
from jax.sharding import PartitionSpec as P

ORBS = 4
SLOTS = 5
LANES = 128
MIB = 1024 * 1024
STEPS = ((0, 0), (-1, 0), (1, 0), (0, -1), (0, 1))
SENT = {
    1: ((4, 7), (6, 8)),
    2: ((4, 1), (0, 2)),
    3: ((4, 5, 2, 8),),
    4: ((4, 3, 0, 6),),
}
ORDER = (0, 3, 4, 1, 2)
EARLY = (0, 1, 2)


def tile_of(i, j):
    da = STEPS[j][0] - STEPS[i][0]
    db = STEPS[j][1] - STEPS[i][1]
    if abs(da) > 1 or abs(db) > 1:
        return None
    return (da + 1) * 3 + db + 1


PAIRS = [
    (ORDER[p], ORDER[q])
    for p in range(SLOTS)
    for q in range(p, SLOTS)
    if tile_of(ORDER[p], ORDER[q]) is not None
]
EARLY_PAIRS = [pair for pair in PAIRS if pair[0] in EARLY and pair[1] in EARLY]
LATE_PAIRS = [pair for pair in PAIRS if pair not in EARLY_PAIRS]


def runs(blocks):
    found = []
    for k in blocks:
        if found and found[-1][1] == k:
            found[-1][1] = k + 1
        else:
            found.append([k, k + 1])
    return found


def added(old, new):
    return new if old is None else old + new


class Halo:
    def __init__(self, slots, potential, own, received):
        self.own, self.received = own, received
        blk = own.shape[-1]
        rows = lax.broadcasted_iota(jnp.int32, (blk, blk), 0)
        self.eye = rows == lax.broadcasted_iota(jnp.int32, (blk, blk), 1)
        self.live = [(slots[0, i] >= 0).astype(jnp.float32) for i in range(SLOTS)]
        self.potential = potential[0, 0]
        self.row_sums = [None] * SLOTS
        self.col_sums = [None] * SLOTS

    def tile(self, i, j):
        k = tile_of(i, j)
        if i == 0:
            return self.own[0, k]
        for part, group in zip(self.received[i], SENT[i]):
            if k in group:
                return part[0, group.index(k)]

    def block(self, i, j):
        both = self.tile(i, j).astype(jnp.float32) + self.tile(j, i).T.astype(jnp.float32)
        if i == j:
            block = (jnp.where(self.eye, self.potential, 0.0) - 0.5 * both) * self.live[i]
        else:
            block = both * (-0.5 * self.live[i] * self.live[j])
        squares = block * block
        folded = squares[:, :LANES]
        for lane in range(LANES, squares.shape[1], LANES):
            folded = folded + squares[:, lane : lane + LANES]
        self.row_sums[i] = added(self.row_sums[i], folded)
        if i != j:
            self.col_sums[j] = added(self.col_sums[j], jnp.sum(squares, axis=0, keepdims=True))
        return block

    def sums(self, i):
        total = self.row_sums[i]
        if total is not None:
            total = jnp.sum(total, axis=1, keepdims=True)
        if self.col_sums[i] is not None:
            turned = jnp.sum(jnp.where(self.eye, self.col_sums[i], 0.0), axis=1, keepdims=True)
            total = added(total, turned)
        return total


def early_kernel(slots, potential, own, r1a, r2a, blocks, sums):
    halo = Halo(slots, potential, own, {1: (r1a,), 2: (r2a,)})
    for place, (i, j) in enumerate(EARLY_PAIRS):
        blocks[place] = halo.block(i, j)
    lane = lax.broadcasted_iota(jnp.int32, sums.shape, 1)
    total = jnp.zeros(sums.shape, jnp.float32)
    for i in EARLY:
        total = jnp.where(lane == i, halo.sums(i), total)
    sums[...] = total


def late_kernel(
    slots, potential, own, early, sums, r1b, r2b, r3, r4, density, charges,
    first, y, x1b, x0, x0b, q0b, out, sems,
):
    blk = own.shape[-1]
    f32, bf16 = jnp.float32, jnp.bfloat16
    halo = Halo(slots, potential, own, {1: (None, r1b), 2: (None, r2b), 3: (r3,), 4: (r4,)})
    eye = halo.eye

    def at(p, q=None):
        return slice(p * blk, (p + 1 if q is None else q) * blk)

    def coupled(p, q):
        return tile_of(ORDER[p], ORDER[q]) is not None

    def product(left, right, p, q):
        total = None
        full = right is x0b
        inner = [
            k for k in range(SLOTS)
            if (left is not x0b or coupled(p, k)) and (not full or coupled(k, q))
        ]
        for lo, hi in runs([k for k in inner if full or k <= q]):
            term = jnp.dot(left[at(p), at(lo, hi)], right[at(lo, hi), at(q)], preferred_element_type=f32)
            total = added(total, term)
        for lo, hi in runs([k for k in inner if not full and k > q]):
            term = lax.dot_general(
                left[at(p), at(lo, hi)], right[at(q), at(lo, hi)],
                (((1,), (1,)), ((), ())), preferred_element_type=f32,
            )
            total = added(total, term)
        return total

    def mirror(target, p, q, block):
        rounded = block.astype(bf16)
        target[at(p), at(q)] = rounded
        if p != q:
            target[at(q), at(p)] = rounded.T

    def place(i, j):
        return ORDER.index(i), ORDER.index(j)

    for n, (i, j) in enumerate(LATE_PAIRS):
        x0[n] = halo.block(i, j)
    largest = None
    for i in range(SLOTS):
        total = halo.sums(i)
        if i in EARLY:
            total = added(sums[:, i : i + 1], total) if total is not None else sums[:, i : i + 1]
        top = jnp.max(total, axis=0, keepdims=True)
        largest = top if largest is None else jnp.maximum(largest, top)
    inv = 1.0 / (2.0 * jnp.sqrt(largest + 1e-06))

    def unscaled(i, j):
        if (i, j) in EARLY_PAIRS:
            return early[EARLY_PAIRS.index((i, j))]
        return x0[LATE_PAIRS.index((i, j))]

    for i, j in PAIRS:
        mirror(x0b, *place(i, j), unscaled(i, j) * inv)
    linear = 1.5 * inv
    upper = [(p, q) for p in range(SLOTS) for q in range(p, SLOTS)]
    for p, q in upper:
        q0b[at(p), at(q)] = product(x0b, x0b, p, q).astype(bf16)
    for p, q in upper:
        block = -0.5 * product(x0b, q0b, p, q)
        if coupled(p, q):
            block = linear * unscaled(ORDER[p], ORDER[q]) + block
        if p == 0:
            first[:, at(q)] = block
        x1b[at(p), at(q)] = block.astype(bf16)
    for q in range(SLOTS):
        y[:, at(q)] = product(x1b, x1b, 0, q).astype(bf16)
    copies = []
    for q in range(SLOTS):
        sign = 1.5 * first[:, at(q)] - 0.5 * product(y, x1b, 0, q)
        if q == 0:
            sign = jnp.where(eye, 1.0 + sign, sign)
        result = 0.5 * sign
        out[q] = result
        copy = pltpu.make_async_copy(
            out.at[q], density.at[0, :, pl.ds(ORDER[q] * blk, blk)], sems.at[q]
        )
        copy.start()
        copies.append(copy)
        if q == 0:
            occupied = jnp.sum(jnp.where(eye, result, 0.0), axis=1, keepdims=True)
            lanes = charges.shape[1]
            atoms = blk // ORBS
            half = slots[0, 0] % 2
            atom = lax.broadcasted_iota(jnp.int32, (blk, lanes), 0) // ORBS + half * atoms
            lane = lax.broadcasted_iota(jnp.int32, (blk, lanes), 1)
            charges[...] = jnp.sum(
                jnp.where(atom == lane, 4.0 / ORBS - 2.0 * occupied, 0.0), axis=0, keepdims=True
            )
    for copy in copies:
        copy.wait()


VMEM = pl.BlockSpec(memory_space=pltpu.VMEM)
SMEM = pl.BlockSpec(memory_space=pltpu.SMEM)
ANY = pl.BlockSpec(memory_space=pl.ANY)


SMALL = pl.CostEstimate(flops=1, bytes_accessed=1, transcendentals=0)


LIMIT = pltpu.CompilerParams(vmem_limit_bytes=20 * MIB)


def early_part(slots, potential, own, r1a, r2a):
    blk = own.shape[-1]
    return pl.pallas_call(
        early_kernel,
        out_shape=(
            jax.ShapeDtypeStruct((len(EARLY_PAIRS), blk, blk), jnp.float32),
            jax.ShapeDtypeStruct((blk, LANES), jnp.float32),
        ),
        in_specs=[SMEM, SMEM] + [VMEM] * 3,
        out_specs=(VMEM, VMEM),
        compiler_params=LIMIT,
        cost_estimate=SMALL,
        name="early_blocks",
    )(slots, potential, own, r1a, r2a)


def late_part(slots, potential, own, early, sums, r1b, r2b, r3, r4):
    blk = own.shape[-1]
    order = SLOTS * blk
    return pl.pallas_call(
        late_kernel,
        out_shape=(
            jax.ShapeDtypeStruct((1, blk, order), jnp.float32),
            jax.ShapeDtypeStruct((1, LANES), jnp.float32),
        ),
        in_specs=[SMEM, SMEM] + [VMEM] * 7,
        out_specs=(ANY, VMEM),
        scratch_shapes=[
            pltpu.VMEM((blk, order), jnp.float32),
            pltpu.VMEM((blk, order), jnp.bfloat16),
            pltpu.VMEM((order, order), jnp.bfloat16),
            pltpu.VMEM((len(LATE_PAIRS), blk, blk), jnp.float32),
            pltpu.VMEM((order, order), jnp.bfloat16),
            pltpu.VMEM((order, order), jnp.bfloat16),
            pltpu.VMEM((SLOTS, blk, blk), jnp.float32),
            pltpu.SemaphoreType.DMA((SLOTS,)),
        ],
        compiler_params=LIMIT,
        name="density_rows",
    )(slots, potential, own, early, sums, r1b, r2b, r3, r4)


def pack_kernel(groups, own, earlier, *packs):
    for group, pack in zip(groups, packs):
        for index, k in enumerate(group):
            pack[0, index] = own[0, k]


def packed(own, earlier, *groups):
    blk = own.shape[-1]
    return pl.pallas_call(
        functools.partial(pack_kernel, groups),
        out_shape=tuple(
            jax.ShapeDtypeStruct((1, len(group), blk, blk), own.dtype) for group in groups
        ),
        in_specs=[VMEM, ANY],
        out_specs=(VMEM,) * len(groups),
        compiler_params=LIMIT,
        cost_estimate=SMALL,
        name="pack_halo",
    )(own, earlier)


def pair_kernel(rows, out):
    half = out.shape[0]
    out[...] = rows[pl.ds(0, half, stride=2), :] + rows[pl.ds(1, half, stride=2), :]


def paired(rows):
    return pl.pallas_call(
        pair_kernel,
        out_shape=jax.ShapeDtypeStruct((rows.shape[0] // 2, rows.shape[1]), rows.dtype),
        in_specs=[VMEM],
        out_specs=VMEM,
        compiler_params=LIMIT,
        name="pair_charges",
    )(rows)


def shards(hamiltonian, partitions, chemical_potential):
    n_dom, n_sub = lax.axis_size("dom"), lax.axis_size("sub")
    potential = chemical_potential.reshape(1, 1)

    def up(x, axis, size):
        return lax.ppermute(x, axis, [(i, (i + 1) % size) for i in range(size)])

    def down(x, axis, size):
        return lax.ppermute(x, axis, [((i + 1) % size, i) for i in range(size)])

    sub_up, sub_down, dom_first = packed(
        hamiltonian, hamiltonian, *SENT[3], *SENT[4], SENT[1][0]
    )
    dom_parts = packed(hamiltonian, sub_up, SENT[1][1], *SENT[2])
    r3 = up(sub_up, "sub", n_sub)
    r4 = down(sub_down, "sub", n_sub)
    r1a, r1b = [up(x, "dom", n_dom) for x in (dom_first, dom_parts[0])]
    r2a, r2b = [down(x, "dom", n_dom) for x in dom_parts[1:]]
    early, sums = early_part(partitions, potential, hamiltonian, r1a, r2a)
    density, row = late_part(
        partitions, potential, hamiltonian, early, sums, r1b, r2b, r3, r4
    )
    copies = jnp.broadcast_to(row, (n_dom * n_sub, LANES))
    rows = lax.all_to_all(copies, ("dom", "sub"), 0, 0, tiled=True)
    return (density, paired(rows).reshape(-1))


def solution(mesh):
    return jax.shard_map(
        shards,
        mesh=mesh,
        in_specs=(P(("dom", "sub"), None, None, None), P(("dom", "sub"), None), P()),
        out_specs=(P(("dom", "sub"), None, None), P()),
        check_vma=False,
    )
```

```python
import functools

import jax
import jax.numpy as jnp
from jax import lax
from jax.experimental import pallas as pl
from jax.experimental.pallas import tpu as pltpu
from jax.sharding import PartitionSpec as P

ORBS = 4
SLOTS = 5
LANES = 128
MIB = 1024 * 1024
STEPS = ((0, 0), (-1, 0), (1, 0), (0, -1), (0, 1))
SENT = {
    1: ((4, 7), (6, 8)),
    2: ((4, 1), (0, 2)),
    3: ((4, 5, 2, 8),),
    4: ((4, 3, 0, 6),),
}
ORDER = (0, 3, 4, 1, 2)
EARLY = (0, 1, 2)


def tile_of(i, j):
    da = STEPS[j][0] - STEPS[i][0]
    db = STEPS[j][1] - STEPS[i][1]
    if abs(da) > 1 or abs(db) > 1:
        return None
    return (da + 1) * 3 + db + 1


PAIRS = [
    (ORDER[p], ORDER[q])
    for p in range(SLOTS)
    for q in range(p, SLOTS)
    if tile_of(ORDER[p], ORDER[q]) is not None
]
EARLY_PAIRS = [pair for pair in PAIRS if pair[0] in EARLY and pair[1] in EARLY]
LATE_PAIRS = [pair for pair in PAIRS if pair not in EARLY_PAIRS]


def runs(blocks):
    found = []
    for k in blocks:
        if found and found[-1][1] == k:
            found[-1][1] = k + 1
        else:
            found.append([k, k + 1])
    return found


def added(old, new):
    return new if old is None else old + new


class Halo:
    def __init__(self, slots, potential, own, received):
        self.own, self.received = own, received
        blk = own.shape[-1]
        rows = lax.broadcasted_iota(jnp.int32, (blk, blk), 0)
        self.eye = rows == lax.broadcasted_iota(jnp.int32, (blk, blk), 1)
        self.live = [(slots[0, i] >= 0).astype(jnp.float32) for i in range(SLOTS)]
        self.potential = potential[0, 0]
        self.row_sums = [None] * SLOTS
        self.col_sums = [None] * SLOTS

    def tile(self, i, j):
        k = tile_of(i, j)
        if i == 0:
            return self.own[0, k]
        for part, group in zip(self.received[i], SENT[i]):
            if k in group:
                return part[0, group.index(k)]

    def block(self, i, j):
        half = 0.5 * self.live[i] if i == j else -0.5 * self.live[i] * self.live[j]
        both = half * self.tile(i, j).astype(jnp.float32) + half * self.tile(j, i).T.astype(jnp.float32)
        block = both
        if i == j:
            block = jnp.where(self.eye, self.potential * self.live[i], 0.0) - both
        squares = block * block
        folded = squares[:, :LANES]
        for lane in range(LANES, squares.shape[1], LANES):
            folded = folded + squares[:, lane : lane + LANES]
        self.row_sums[i] = added(self.row_sums[i], folded)
        if i != j:
            self.col_sums[j] = added(self.col_sums[j], jnp.sum(squares, axis=0, keepdims=True))
        return block

    def sums(self, i):
        total = self.row_sums[i]
        if total is not None:
            total = jnp.sum(total, axis=1, keepdims=True)
        if self.col_sums[i] is not None:
            turned = jnp.sum(jnp.where(self.eye, self.col_sums[i], 0.0), axis=1, keepdims=True)
            total = added(total, turned)
        return total


def early_kernel(slots, potential, own, r1a, r2a, blocks, sums):
    halo = Halo(slots, potential, own, {1: (r1a,), 2: (r2a,)})
    for place, (i, j) in enumerate(EARLY_PAIRS):
        blocks[place] = halo.block(i, j)
    lane = lax.broadcasted_iota(jnp.int32, sums.shape, 1)
    total = jnp.zeros(sums.shape, jnp.float32)
    for i in EARLY:
        total = jnp.where(lane == i, halo.sums(i), total)
    sums[...] = total


def late_kernel(
    slots, potential, own, early, sums, r1b, r2b, r3, r4, density, charges,
    first, y, x1b, x0, x0b, q0b, out, sems,
):
    blk = own.shape[-1]
    f32, bf16 = jnp.float32, jnp.bfloat16
    halo = Halo(slots, potential, own, {1: (None, r1b), 2: (None, r2b), 3: (r3,), 4: (r4,)})
    eye = halo.eye

    def at(p, q=None):
        return slice(p * blk, (p + 1 if q is None else q) * blk)

    def coupled(p, q):
        return tile_of(ORDER[p], ORDER[q]) is not None

    def product(left, right, p, q):
        total = None
        full = right is x0b
        inner = [
            k for k in range(SLOTS)
            if (left is not x0b or coupled(p, k)) and (not full or coupled(k, q))
        ]
        for lo, hi in runs([k for k in inner if full or k <= q]):
            term = jnp.dot(left[at(p), at(lo, hi)], right[at(lo, hi), at(q)], preferred_element_type=f32)
            total = added(total, term)
        for lo, hi in runs([k for k in inner if not full and k > q]):
            term = lax.dot_general(
                left[at(p), at(lo, hi)], right[at(q), at(lo, hi)],
                (((1,), (1,)), ((), ())), preferred_element_type=f32,
            )
            total = added(total, term)
        return total

    def mirror(target, p, q, block):
        rounded = block.astype(bf16)
        target[at(p), at(q)] = rounded
        if p != q:
            target[at(q), at(p)] = rounded.T

    def place(i, j):
        return ORDER.index(i), ORDER.index(j)

    for n, (i, j) in enumerate(LATE_PAIRS):
        x0[n] = halo.block(i, j)
    largest = None
    for i in range(SLOTS):
        total = halo.sums(i)
        if i in EARLY:
            total = added(sums[:, i : i + 1], total) if total is not None else sums[:, i : i + 1]
        top = jnp.max(total, axis=0, keepdims=True)
        largest = top if largest is None else jnp.maximum(largest, top)
    inv = 1.0 / (2.0 * jnp.sqrt(largest + 1e-06))

    def unscaled(i, j):
        if (i, j) in EARLY_PAIRS:
            return early[EARLY_PAIRS.index((i, j))]
        return x0[LATE_PAIRS.index((i, j))]

    for i, j in PAIRS:
        mirror(x0b, *place(i, j), unscaled(i, j) * inv)
    linear = 1.5 * inv
    upper = [(p, q) for p in range(SLOTS) for q in range(p, SLOTS)]
    for p, q in upper:
        q0b[at(p), at(q)] = product(x0b, x0b, p, q).astype(bf16)
    for p, q in upper:
        block = -0.5 * product(x0b, q0b, p, q)
        if coupled(p, q):
            block = linear * unscaled(ORDER[p], ORDER[q]) + block
        if p == 0:
            first[:, at(q)] = block
        x1b[at(p), at(q)] = block.astype(bf16)
    for q in range(SLOTS):
        y[:, at(q)] = product(x1b, x1b, 0, q).astype(bf16)
    copies = []
    for q in range(SLOTS):
        sign = 1.5 * first[:, at(q)] - 0.5 * product(y, x1b, 0, q)
        if q == 0:
            sign = jnp.where(eye, 1.0 + sign, sign)
        result = 0.5 * sign
        out[q] = result
        copy = pltpu.make_async_copy(
            out.at[q], density.at[0, :, pl.ds(ORDER[q] * blk, blk)], sems.at[q]
        )
        copy.start()
        copies.append(copy)
        if q == 0:
            occupied = jnp.sum(jnp.where(eye, result, 0.0), axis=1, keepdims=True)
            lanes = charges.shape[1]
            atoms = blk // ORBS
            half = slots[0, 0] % 2
            atom = lax.broadcasted_iota(jnp.int32, (blk, lanes), 0) // ORBS + half * atoms
            lane = lax.broadcasted_iota(jnp.int32, (blk, lanes), 1)
            charges[...] = jnp.sum(
                jnp.where(atom == lane, 4.0 / ORBS - 2.0 * occupied, 0.0), axis=0, keepdims=True
            )
    for copy in copies:
        copy.wait()


VMEM = pl.BlockSpec(memory_space=pltpu.VMEM)
SMEM = pl.BlockSpec(memory_space=pltpu.SMEM)
ANY = pl.BlockSpec(memory_space=pl.ANY)


SMALL = pl.CostEstimate(flops=1, bytes_accessed=1, transcendentals=0)


LIMIT = pltpu.CompilerParams(vmem_limit_bytes=20 * MIB)


def early_part(slots, potential, own, r1a, r2a):
    blk = own.shape[-1]
    return pl.pallas_call(
        early_kernel,
        out_shape=(
            jax.ShapeDtypeStruct((len(EARLY_PAIRS), blk, blk), jnp.float32),
            jax.ShapeDtypeStruct((blk, LANES), jnp.float32),
        ),
        in_specs=[SMEM, SMEM] + [VMEM] * 3,
        out_specs=(VMEM, VMEM),
        compiler_params=LIMIT,
        cost_estimate=SMALL,
        name="early_blocks",
    )(slots, potential, own, r1a, r2a)


def late_part(slots, potential, own, early, sums, r1b, r2b, r3, r4):
    blk = own.shape[-1]
    order = SLOTS * blk
    return pl.pallas_call(
        late_kernel,
        out_shape=(
            jax.ShapeDtypeStruct((1, blk, order), jnp.float32),
            jax.ShapeDtypeStruct((1, LANES), jnp.float32),
        ),
        in_specs=[SMEM, SMEM] + [VMEM] * 7,
        out_specs=(ANY, VMEM),
        scratch_shapes=[
            pltpu.VMEM((blk, order), jnp.float32),
            pltpu.VMEM((blk, order), jnp.bfloat16),
            pltpu.VMEM((order, order), jnp.bfloat16),
            pltpu.VMEM((len(LATE_PAIRS), blk, blk), jnp.float32),
            pltpu.VMEM((order, order), jnp.bfloat16),
            pltpu.VMEM((order, order), jnp.bfloat16),
            pltpu.VMEM((SLOTS, blk, blk), jnp.float32),
            pltpu.SemaphoreType.DMA((SLOTS,)),
        ],
        compiler_params=LIMIT,
        name="density_rows",
    )(slots, potential, own, early, sums, r1b, r2b, r3, r4)


def pack_kernel(groups, own, earlier, *packs):
    for group, pack in zip(groups, packs):
        for index, k in enumerate(group):
            pack[0, index] = own[0, k]


def packed(own, earlier, *groups):
    blk = own.shape[-1]
    return pl.pallas_call(
        functools.partial(pack_kernel, groups),
        out_shape=tuple(
            jax.ShapeDtypeStruct((1, len(group), blk, blk), own.dtype) for group in groups
        ),
        in_specs=[VMEM, ANY],
        out_specs=(VMEM,) * len(groups),
        compiler_params=LIMIT,
        cost_estimate=SMALL,
        name="pack_halo",
    )(own, earlier)


def pair_kernel(rows, out):
    half = out.shape[0]
    out[...] = rows[pl.ds(0, half, stride=2), :] + rows[pl.ds(1, half, stride=2), :]


def paired(rows):
    return pl.pallas_call(
        pair_kernel,
        out_shape=jax.ShapeDtypeStruct((rows.shape[0] // 2, rows.shape[1]), rows.dtype),
        in_specs=[VMEM],
        out_specs=VMEM,
        compiler_params=LIMIT,
        name="pair_charges",
    )(rows)


def shards(hamiltonian, partitions, chemical_potential):
    n_dom, n_sub = lax.axis_size("dom"), lax.axis_size("sub")
    potential = chemical_potential.reshape(1, 1)

    def up(x, axis, size):
        return lax.ppermute(x, axis, [(i, (i + 1) % size) for i in range(size)])

    def down(x, axis, size):
        return lax.ppermute(x, axis, [((i + 1) % size, i) for i in range(size)])

    sub_up, sub_down, dom_first = packed(
        hamiltonian, hamiltonian, *SENT[3], *SENT[4], SENT[1][0]
    )
    dom_parts = packed(hamiltonian, sub_up, SENT[1][1], *SENT[2])
    r3 = up(sub_up, "sub", n_sub)
    r4 = down(sub_down, "sub", n_sub)
    r1a, r1b = [up(x, "dom", n_dom) for x in (dom_first, dom_parts[0])]
    r2a, r2b = [down(x, "dom", n_dom) for x in dom_parts[1:]]
    early, sums = early_part(partitions, potential, hamiltonian, r1a, r2a)
    density, row = late_part(
        partitions, potential, hamiltonian, early, sums, r1b, r2b, r3, r4
    )
    copies = jnp.broadcast_to(row, (n_dom * n_sub, LANES))
    rows = lax.all_to_all(copies, ("dom", "sub"), 0, 0, tiled=True)
    return (density, paired(rows).reshape(-1))


def solution(mesh):
    return jax.shard_map(
        shards,
        mesh=mesh,
        in_specs=(P(("dom", "sub"), None, None, None), P(("dom", "sub"), None), P()),
        out_specs=(P(("dom", "sub"), None, None), P()),
        check_vma=False,
    )
```
